512 devices in a mesh: section: 8 (over z_hi, core), dp: 64 (over z_lo, y, x).
Axes of the slice: x: 4, y: 8, z: 8 (z_hi: 4, z_lo: 2; z = z_hi * 2 + z_lo), core: 2. Of those that a mesh axis runs over, the one named last changes fastest.
Arguments:
- patches: bfloat16 [4096, 8, 3200], P('dp'), may hold values from -6 to 6
- tile_counts: int32 [512], P('dp'), may hold values from 1 to 8, as said below
- owners: int32 [4096, 1], P('dp'), may hold values from 0 to 63; in each aligned block of 64 rows (0 to 63, 64 to 127, ...) at most 2 rows name the same one
- plan: int32 [8, 4], replicated, may hold values from 0 to 31, as said below
- norm_gain: float32 [3200], replicated, may hold values from 0.25 to 1.75
- fc1_weight: bfloat16 [3200, 6400], P('dp', 'section'), may hold values from -0.109375 to 0.109375
- fc1_bias: float32 [6400], replicated, may hold values from -4 to 4
- fc2_weight: bfloat16 [6400, 3200], P('section', 'dp'), may hold values from -0.078125 to 0.078125
- fc2_bias: float32 [3200], replicated, may hold values from -3 to 3
- layer_scale: float32 [3200], replicated, may hold values from 0.3 to 3
Outputs:
- received: bfloat16 [65536, 3200], P('dp', 'section')
The draws below stay inside these ranges and needn't reach their ends.
Inputs may be any that keep to these rules, and one draw needn't show every extreme that they name: `tile_counts`: every dp index has an image with 8 tiles. `owners`: at most 2 tile slots of one dp index name one owner. `plan`: a permutation of the hidden-unit blocks.
All inputs are finite; a program needn't handle non-finite values.
Results may differ from the reference program's by a relative error of at most 0.015.
Values may be sent and summed in bfloat16 or wider, within the bound.
A program may use at most 128 MiB of HBM per device.

```python
import math
import jax
import jax.numpy as jnp
import numpy as np
from jax import lax

D = 3200
FF = 6400
IMG_DEV = 8
MAX_TILES = 8
TILE_ROWS = 8
SLOTS = 4
TILES_DEV = 64
TILES = 4096
IMAGES = 512
CAP = 2
N_SECTION = 8
N_DP = 64


def draw_tile_counts(key, part):
    key = jax.random.fold_in(key, 11)
    low_key, count_key = jax.random.split(key)
    floor_level = jax.random.randint(low_key, (N_DP, 1), 1, MAX_TILES + 1)
    spread = jax.random.randint(count_key, (N_DP, IMG_DEV), 0, MAX_TILES + 1)
    counts = jnp.minimum(floor_level + spread // 2, MAX_TILES)
    first = jnp.arange(IMG_DEV)[None, :] == 0
    counts = jnp.where(first, MAX_TILES, counts)
    return counts.reshape(IMAGES).astype(jnp.int32)


def draw_plan(key, part):
    key = jax.random.fold_in(key, 23)
    order = jax.random.permutation(key, N_SECTION * SLOTS)
    return order.reshape(N_SECTION, SLOTS).astype(jnp.int32)


def shard_levels(stream_key, shape, pieces, least, top_value):
    def one(position, parts):
        steps = jax.random.uniform(jax.random.fold_in(jax.random.fold_in(stream_key, 6), position), (parts,), jnp.float32, least / len(pieces), top_value / len(pieces))
        return jnp.repeat(jnp.exp(steps), shape[position] // parts).reshape((-1,) + (1,) * (len(shape) - position - 1))

    factor_of = one(*pieces[0])
    for cut in pieces[1:]:
        factor_of = factor_of * one(*cut)
    return factor_of


def assign_block(rng, own, number, rows, count, top, most, slope):
    ranking = jax.random.permutation(rng, count)
    heavy_load, common = shares(count, rows * top, most, slope, True), shares(count, rows * top, most, slope, False)
    places = jnp.arange(count)

    def named(sizes, rotation):
        used = int((sizes > 0).sum())
        fixed = max(1, used // 4)
        moved = fixed + (places - fixed + rotation * (used - fixed)) % max(1, count - fixed)
        return jnp.zeros((count,), jnp.int32).at[ranking[jnp.where(places < fixed, places, moved)]].set(jnp.asarray(sizes, jnp.int32))

    sizes = jnp.where(number % 4 == 0, named(heavy_load, number // 4), named(common, number - number // 4 - 1))
    mixed = jax.random.permutation(jax.random.fold_in(own, 3), count)
    donor, sink = mixed[0:count // 2 * 2:2], mixed[1:count // 2 * 2:2]
    margin = jnp.minimum(sizes[donor] - 1, most - sizes[sink]) // 2
    margin = jnp.where((donor == ranking[0]) | (sink == ranking[0]) | (sizes[sink] == 0), 0, jnp.maximum(margin, 0))
    moved = jax.random.randint(jax.random.fold_in(own, 4), (count // 2,), 0, 1 << 20) % (margin + 1)
    sizes = sizes.at[donor].add(-moved).at[sink].add(moved)
    labels = jnp.searchsorted(jnp.cumsum(sizes), jnp.arange(rows * top), side="right").astype(jnp.int32)
    grid = labels.reshape(top, rows).T
    grid = grid[jax.random.permutation(jax.random.fold_in(own, 1), rows)]
    rotation = jax.random.randint(jax.random.fold_in(own, 2), (rows, 1), 0, top)
    return jnp.take_along_axis(grid, (jnp.arange(top)[None, :] + rotation) % top, axis=1)


def shares(amount, total, reach, skew, full):
    portions = [(1 << 20) // math.isqrt(rank ** skew) + 1 for rank in range(1, amount + 1)]
    largest = reach if full else min(reach, max(-(-total // amount), total * portions[0] // sum(portions)))
    least = 1 if total - largest >= amount - 1 else 0
    given, surplus = [largest] + [least] * (amount - 1), total - largest - least * (amount - 1)
    while surplus > 0:
        movable = [i for i in range(1, amount) if given[i] < largest] or [i for i in range(1, amount) if given[i] < reach]
        pool, remaining = sum([portions[i] for i in movable]), surplus
        for i in movable:
            addition = min(reach - given[i], max(1, remaining * portions[i] // pool), surplus)
            given[i] = given[i] + addition
            surplus = surplus - addition
    return np.array(given)


def noise(own_key, dims, deviation, reach, cuts=(), held_as=jnp.bfloat16):
    drawn = jax.random.normal(own_key, dims, jnp.float32) * deviation
    if len(cuts) > 0:
        drawn = shard_levels(own_key, dims, cuts, -0.22, 0.18) * drawn
    return jnp.clip(drawn, min=-reach, max=reach).astype(held_as)


def setup_inputs(seed: int = 0) -> dict:
    key_of = jax.random.split(jax.random.key(seed), 11)
    patches = noise(key_of[0], (TILES, TILE_ROWS, D), 1.0, 6.0, ((0, 64),))
    tile_counts = draw_tile_counts(jax.random.fold_in(key_of[10], 71), 0)
    owners_keys = jax.random.split(jax.random.fold_in(key_of[2], 1), TILES // TILES_DEV)
    owners_turns = jax.random.permutation(jax.random.fold_in(key_of[2], 3), TILES // TILES_DEV)
    owners = jax.vmap(lambda own, number: assign_block(jax.random.fold_in(key_of[2], 2), own, number, TILES_DEV, N_DP, 1, CAP, 2))(owners_keys, owners_turns).reshape((TILES, 1))
    plan = draw_plan(jax.random.fold_in(key_of[10], 71), 0)
    norm_gain = jnp.clip(1.0 + 0.15 * jax.random.normal(key_of[4], (D,), jnp.float32), 0.25, 1.75)
    fc1_weight = noise(key_of[5], (D, FF), D ** -0.5, 0.109375, ((0, 64), (1, 8)))
    fc1_bias = noise(key_of[6], (FF,), 1.0, 4.0, (), jnp.float32)
    fc2_weight = noise(key_of[7], (FF, D), FF ** -0.5, 0.078125, ((0, 8), (1, 64)))
    fc2_bias = noise(key_of[8], (D,), 0.5, 3.0, (), jnp.float32)
    layer_scale = jnp.clip(jnp.exp(jax.random.uniform(key_of[9], (D,), jnp.float32, math.log(0.3), math.log(3.0))), 0.3, 3.0)
    return dict(patches=patches, tile_counts=tile_counts, owners=owners, plan=plan, norm_gain=norm_gain, fc1_weight=fc1_weight, fc1_bias=fc1_bias, fc2_weight=fc2_weight, fc2_bias=fc2_bias, layer_scale=layer_scale)


def reference(patches, tile_counts, owners, plan, norm_gain, fc1_weight, fc1_bias, fc2_weight, fc2_bias, layer_scale):
    block_width = FF // (N_SECTION * SLOTS)
    section_width = FF // N_SECTION
    loc_bias = jnp.take(fc1_bias.reshape(N_SECTION * SLOTS, block_width), plan.reshape(-1), axis=0).reshape(FF)
    tiles_dev = IMG_DEV * MAX_TILES
    alive = (jnp.arange(MAX_TILES)[None, :] < tile_counts[:, None]).reshape(N_DP, tiles_dev)
    blocks = patches.reshape(N_DP, tiles_dev * TILE_ROWS, D)

    def encode(pair):
        rows, live = pair
        values = rows.astype(jnp.float32)
        scale = lax.rsqrt(lax.optimization_barrier(jnp.mean(values * values, axis=1, keepdims=True)) + 1e-06)
        normed = (values * scale * norm_gain).astype(jnp.bfloat16)
        pre = jnp.dot(normed, fc1_weight, preferred_element_type=jnp.float32) + loc_bias
        hidden = jax.nn.gelu(pre, approximate=False).astype(jnp.bfloat16)
        branch = jnp.zeros((rows.shape[0], D), jnp.float32)
        for section_pos in range(N_SECTION):
            lo = section_pos * section_width
            term = jnp.dot(hidden[:, lo:lo + section_width], fc2_weight[lo:lo + section_width], preferred_element_type=jnp.float32)
            term = lax.optimization_barrier(term.astype(jnp.bfloat16))
            branch = branch + term.astype(jnp.float32)
        branch = branch + fc2_bias
        keep = jnp.repeat(live, TILE_ROWS).astype(jnp.float32)[:, None]
        return ((values + layer_scale * branch) * keep).astype(jnp.bfloat16)
    encoded = lax.map(encode, (blocks, alive))
    owner = owners[:, 0].reshape(N_DP, tiles_dev).astype(jnp.int32)
    same = owner[:, :, None] == owner[:, None, :]
    earlier = jnp.arange(tiles_dev)[:, None] > jnp.arange(tiles_dev)[None, :]
    rank = lax.optimization_barrier(jnp.sum((same & earlier[None]).astype(jnp.int32), axis=2)).astype(jnp.int32)
    source = jnp.arange(N_DP, dtype=jnp.int32)[:, None]
    target = ((owner * N_DP + source) * CAP + rank).reshape(-1).astype(jnp.int32)
    result = jnp.zeros((N_DP * N_DP * CAP, TILE_ROWS, D), jnp.bfloat16)
    result = result.at[target].set(encoded.reshape(N_DP * tiles_dev, TILE_ROWS, D))
    return result.reshape(N_DP * N_DP * CAP * TILE_ROWS, D)
```

```python
import jax
import jax.numpy as jnp
from jax import lax
from jax.experimental import pallas as pl
from jax.experimental.pallas import tpu as pltpu
from jax.sharding import PartitionSpec as P

MESH = pl.DeviceIdType.MESH
F32 = jnp.float32
BF16 = jnp.bfloat16

NQ, NC, NZ, NY, NX = 4, 2, 2, 8, 4
NS = NQ * NC
D = 3200
FF = 800
FP = 896
SH = 50
SHP = 64
RUN = 200
RUNP = 208
FEAT = 400
ROWS = 512
TOK = 256
CUTS = ((0, 512), (512, 384))


def md(a, n):
    return lax.rem(a, jnp.int32(n))


def dv(a, n):
    return lax.div(a, jnp.int32(n))


def dot(a, b, dims=((1,), (0,))):
    return lax.dot_general(a, b, (dims, ((), ())), preferred_element_type=F32)


def iota(shape, dim):
    return lax.broadcasted_iota(jnp.int32, shape, dim)


def window(start):
    block = dv(start, 128) - dv(start, 3000)
    return pl.multiple_of(block * 128, 128), start - block * 128


def kernel(
    patches,
    gain,
    w1,
    w2,
    loc_bias,
    own_scale,
    own_bias,
    target,
    out,
    own,
    stage,
    wall,
    normed,
    acts,
    acc,
    hidden,
    part,
    pair,
    ring_out,
    ring_in,
    branch,
    encoded,
    going,
    coming,
    turned,
    st_send,
    st_recv,
    y_send,
    y_recv,
    x_send,
    x_recv,
    c_send,
    c_recv,
    r_send,
    r_recv,
    a_send,
    a_recv,
    b_send,
    b_recv,
):
    s = lax.axis_index("section")
    d = lax.axis_index("dp")
    q, c = dv(s, 2), md(s, 2)
    z, y, x = dv(d, 32), md(dv(d, 4), 8), md(d, 4)
    h = md(x, 2)
    e = md(x + z, 2)

    def dp_id(z_, y_, x_):
        return (s, z_ * 32 + y_ * 4 + x_)

    def peer(step):
        g = md(z * 4 + x + step, 8)
        return g, dv(g, 4), md(g, 4)

    def copy(src, dst, send, recv, device):
        return pltpu.make_async_remote_copy(
            src_ref=src,
            dst_ref=dst,
            send_sem=send,
            recv_sem=recv,
            device_id=device,
            device_id_type=MESH,
        )

    mate = (q * 2 + 1 - c, d)
    q_up = (md(q + 1, NQ) * 2 + c, d)
    q_dn = (md(q + NQ - 1, NQ) * 2 + c, d)

    barrier = pltpu.get_barrier_semaphore()
    for step in range(1, 8):
        _, zp, xp = peer(step)
        for device in (dp_id(zp, y, xp), dp_id(z, md(y + step, 8), x)):
            pl.semaphore_signal(barrier, inc=1, device_id=device, device_id_type=MESH)
    for device in (mate, q_up, q_dn):
        pl.semaphore_signal(barrier, inc=1, device_id=device, device_id_type=MESH)

    own[...] = jnp.zeros_like(own)
    own[0, 0:SH, 0:FF] = w1[...]
    eye = (iota((SHP, SH), 0) == iota((SHP, SH), 1)).astype(BF16)
    own[1, :, 0:FF] = dot(eye, w2[...], ((1,), (1,))).astype(BF16)

    pl.semaphore_wait(barrier, 17)

    def stage_copy(m, k, l):
        return copy(
            own.at[m],
            stage.at[m, x],
            st_send.at[m, 2 * k + l],
            st_recv.at[m, x],
            dp_id(md(z + l, 2), y, md(x + e + 2 * k, 4)),
        )

    def stage_start(m):
        for k in range(2):
            for l in range(2):
                if k or l:
                    stage_copy(m, k, l).start()
        pl.when(e == 1)(lambda: stage_copy(m, 0, 0).start())

        @pl.when(e == 0)
        def _():
            stage[m, x] = own[m]

    def stage_arrive(m, j):
        xs = md(x + j, 4)
        copy(own.at[m], stage.at[m, xs], st_send.at[m, 0], st_recv.at[m, xs], dp_id(z, y, x)).wait_recv()

    def stage_finish(m):
        pl.when(e == 1)(lambda: stage_arrive(m, 0))
        for j in range(1, 4):
            stage_arrive(m, j)
        row, col = iota((RUNP, 4 * SHP), 0), iota((RUNP, 4 * SHP), 1)
        pick = ((col == dv(row, SH) * SHP + md(row, SH)) & (row < RUN)).astype(BF16)
        wall[m, y, h] = dot(pick, stage[m].reshape(4 * SHP, FP)).astype(BF16)

    def y_copy(m, way, t, arriving=False):
        back = t + 1 if arriving else t
        b = md(y + 8 - back, 8) if way == 0 else md(y + back, 8)
        to = md(y + 1, 8) if way == 0 else md(y + 7, 8)
        start, size = (0, FP) if t < 3 else CUTS[way]
        ref = wall.at[m, b, h, :, pl.ds(start, size)]
        return copy(ref, ref, y_send.at[m, way, t], y_recv.at[m, way, t], dp_id(z, to, x))

    def x_copy(m, way, b, arriving=False):
        to = md(x + 1, 4) if way == 0 else md(x + 3, 4)
        half = 1 - h if arriving else h
        ref = wall.at[m, b, half, :, pl.ds(CUTS[way][0], CUTS[way][1])]
        return copy(ref, ref, x_send.at[m, way, b], x_recv.at[m, way, b], dp_id(z, y, to))

    def block_at(way, t):
        return md(y + 8 - t, 8) if way == 0 else md(y + t, 8)

    def send_block(m, t):
        for way in range(2):
            if t > 0:
                y_copy(m, way, t - 1, True).wait_recv()
            if t < 4:
                y_copy(m, way, t).start()
            if t in (0, 4):
                x_copy(m, way, block_at(way, t)).start()
            else:
                for other in range(2):
                    x_copy(m, other, block_at(way, t)).start()

    def use_block(m, t, use):
        def one(way, carry):
            b = md(y + way * t + (1 - way) * (8 - t), 8)
            for other in range(2):
                x_copy(m, other, b, True).wait_recv()
            use(b)
            return carry

        lax.fori_loop(0, 1 if t in (0, 4) else 2, one, 0)

    def fc1(b):
        acc[...] += dot(acts[b], wall[0, b].reshape(2 * RUNP, FP))

    def fc2(b):
        term = dot(wall[1, b].reshape(2 * RUNP, FP), hidden[...], ((1,), (1,))).astype(BF16)
        term = term.reshape(2, RUNP, ROWS)
        sec, j = dv(b, 2), md(b, 2)
        part[sec, j] = term[0]
        part[sec + 4, j] = term[1]

    stage_start(0)
    stage_start(1)

    def norm(i, carry):
        at = pl.ds(pl.multiple_of(i * 64, 64), 64)
        values = patches[at, :].astype(F32)
        scale = lax.rsqrt(jnp.mean(values * values, axis=1, keepdims=True) + 1e-06)
        normed[at, :] = (values * scale * gain[...]).astype(BF16)
        return carry

    def act(b, carry):
        total = None
        for half in range(2):
            at, off = window(half * 1600 + b * RUN)
            row, col = iota((384, 2 * RUNP), 0), iota((384, 2 * RUNP), 1) - half * RUNP
            pick = ((row == col + off) & (col >= 0) & (col < RUN)).astype(BF16)
            term = dot(normed[:, pl.ds(at, 384)], pick)
            total = term if total is None else total + term
        acts[b] = total.astype(BF16)
        return carry

    stage_finish(0)
    send_block(0, 0)
    lax.fori_loop(0, 8, norm, 0)
    lax.fori_loop(0, 8, act, 0)
    acc[...] = jnp.zeros_like(acc)
    stage_finish(1)
    send_block(0, 1)
    send_block(1, 0)
    use_block(0, 0, fc1)
    send_block(0, 2)
    use_block(0, 1, fc1)
    send_block(1, 1)
    send_block(0, 3)
    use_block(0, 2, fc1)
    send_block(0, 4)
    use_block(0, 3, fc1)
    send_block(1, 2)
    use_block(0, 4, fc1)

    def gelu(i, carry):
        at = pl.ds(pl.multiple_of(i * 64, 64), 64)
        pre = acc[at, :] + loc_bias[...]
        hidden[at, :] = (0.5 * pre * (1.0 + lax.erf(pre * 0.7071067811865476))).astype(BF16)
        return carry

    lax.fori_loop(0, 8, gelu, 0)
    use_block(1, 0, fc2)
    send_block(1, 3)
    use_block(1, 1, fc2)
    use_block(1, 2, fc2)
    send_block(1, 4)
    use_block(1, 3, fc2)
    use_block(1, 4, fc2)

    def pair_copy(i):
        return copy(part.at[2 * i + 1 - c], pair.at[i], c_send.at[i], c_recv.at[i], mate)

    for i in range(NQ):
        pair_copy(i).start()

    def chunk(i, way):
        at = slice(way * TOK, way * TOK + TOK)
        return part[2 * i + c, :, :, at].astype(F32) + pair[i, :, :, at].astype(F32)

    def ring_copy(way, k):
        return copy(
            ring_out.at[way, k],
            ring_in.at[way, k],
            r_send.at[way, k],
            r_recv.at[way, k],
            q_up if way == 0 else q_dn,
        )

    for i in range(NQ):
        pair_copy(i).wait()
    for k in range(4):
        for way in range(2):
            i = md(q + 7 - k, NQ) if way == 0 else md(q + 1 + k, NQ)
            total = chunk(i, way)
            if k > 0:
                ring_copy(way, k - 1).wait_recv()
                total = total + ring_in[way, k - 1].astype(F32)
            if k < 3:
                ring_out[way, k] = total.astype(BF16)
                ring_copy(way, k).start()
            else:
                branch[:, :, way * TOK : way * TOK + TOK] = total

    for j in range(2):
        at, off = window(s * FEAT + j * RUN)
        row, col = iota((RUNP, 384), 0), iota((RUNP, 384), 1)
        pick = ((col == row + off) & (row < RUN)).astype(BF16)
        rows = dot(pick, patches[:, pl.ds(at, 384)], ((1,), (1,)))
        encoded[j * RUNP : (j + 1) * RUNP] = (
            rows + own_scale[j] * (branch[j] + own_bias[j])
        ).astype(BF16)

    def place(b, carry):
        pick = (target[...] == iota((ROWS, 128), 1) + b * 128).astype(BF16)
        going[b] = dot(encoded[...], pick).astype(BF16)
        return carry

    lax.fori_loop(0, 8, place, 0)

    def a_copy(step, arriving=False):
        to = md(y + step, 8)
        src = md(y + 8 - step, 8) if arriving else y
        return copy(going.at[to], coming.at[src], a_send.at[step], a_recv.at[step], dp_id(z, to, x))

    for step in (4, 3, 5, 2, 6, 1, 7):
        a_copy(step).start()

    row, col = iota((2 * RUNP, FEAT), 0), iota((2 * RUNP, FEAT), 1)
    keep = (row == col + jnp.where(col >= RUN, RUNP - RUN, 0)).astype(BF16)

    def turn(src, block):
        turned[:, src] = dot(block, keep, ((0,), (0,))).astype(BF16).reshape(8, 16, FEAT)

    turn(y, going[y])
    for step in (1, 7, 2, 6, 3, 5, 4):
        a_copy(step, True).wait_recv()
        src = md(y + 8 - step, 8)
        turn(src, coming[src])

    def b_copy(step, arriving=False):
        g, zp, xp = peer(8 - step) if arriving else peer(step)
        zo, xo = (zp, xp) if arriving else (z, x)
        return copy(turned.at[g], out.at[zo, :, xo], b_send.at[step], b_recv.at[step], dp_id(zp, y, xp))

    for step in range(1, 8):
        b_copy(step).start()
    out[z, :, x] = turned[z * 4 + x]
    for step in range(1, 8):
        b_copy(step, True).wait_recv()

    for m in range(2):
        for k in range(2):
            for l in range(2):
                if k or l:
                    stage_copy(m, k, l).wait_send()
        pl.when(e == 1)(lambda: stage_copy(m, 0, 0).wait_send())
        for way in range(2):
            for t in range(4):
                y_copy(m, way, t).wait_send()
            for b in range(8):
                x_copy(m, way, b).wait_send()
    for way in range(2):
        for k in range(3):
            ring_copy(way, k).wait_send()
    for step in range(1, 8):
        a_copy(step).wait_send()
        b_copy(step).wait_send()


def local(
    patches,
    tile_counts,
    owners,
    plan,
    norm_gain,
    fc1_weight,
    fc1_bias,
    fc2_weight,
    fc2_bias,
    layer_scale,
):
    tiles, tile_rows, width = patches.shape
    section_id = lax.axis_index("section")
    blocks = plan.shape[0] * plan.shape[1]
    my_blocks = lax.dynamic_slice_in_dim(plan, section_id, 1, 0)[0]
    loc_bias = jnp.take(fc1_bias.reshape(blocks, -1), my_blocks, axis=0).reshape(1, FF)
    loc_bias = jnp.pad(loc_bias, ((0, 0), (0, FP - FF)))

    per_image = tiles // tile_counts.shape[0]
    live = (jnp.arange(per_image)[None, :] < tile_counts[:, None]).reshape(tiles)
    owner = owners[:, 0]
    same = owner[:, None] == owner[None, :]
    earlier = jnp.arange(tiles)[:, None] > jnp.arange(tiles)[None, :]
    rank = jnp.sum((same & earlier).astype(jnp.int32), axis=1)
    oz, oy, ox = owner // 32, (owner // 4) % 8, owner % 4
    place = oy * 128 + (oz * 4 + ox) * 16 + rank * 8
    target = place[:, None] + jnp.arange(tile_rows, dtype=jnp.int32)[None, :]
    target = jnp.where(live[:, None], target, -1).reshape(ROWS, 1)

    def mine(vector):
        held = lax.dynamic_slice_in_dim(vector, section_id * FEAT, FEAT, 0).reshape(2, RUN, 1)
        return jnp.pad(held, ((0, 0), (0, RUNP - RUN), (0, 0)))

    vmem = pl.BlockSpec(memory_space=pltpu.VMEM)
    dma = pltpu.SemaphoreType.DMA
    received = pl.pallas_call(
        kernel,
        out_shape=jax.ShapeDtypeStruct((NZ, NY, NX, 16, FEAT), BF16),
        in_specs=[vmem] * 8,
        out_specs=vmem,
        scratch_shapes=[
            pltpu.VMEM((2, SHP, FP), BF16),
            pltpu.VMEM((2, 4, SHP, FP), BF16),
            pltpu.VMEM((2, 8, 2, RUNP, FP), BF16),
            pltpu.VMEM((ROWS, D), BF16),
            pltpu.VMEM((8, ROWS, 2 * RUNP), BF16),
            pltpu.VMEM((ROWS, FP), F32),
            pltpu.VMEM((ROWS, FP), BF16),
            pltpu.VMEM((NS, 2, RUNP, ROWS), BF16),
            pltpu.VMEM((NQ, 2, RUNP, ROWS), BF16),
            pltpu.VMEM((2, 3, 2, RUNP, TOK), BF16),
            pltpu.VMEM((2, 3, 2, RUNP, TOK), BF16),
            pltpu.VMEM((2, RUNP, ROWS), F32),
            pltpu.VMEM((2 * RUNP, ROWS), BF16),
            pltpu.VMEM((8, 2 * RUNP, 128), BF16),
            pltpu.VMEM((8, 2 * RUNP, 128), BF16),
            pltpu.VMEM((8, 8, 16, FEAT), BF16),
            dma((2, 4)),
            dma((2, 4)),
            dma((2, 2, 4)),
            dma((2, 2, 4)),
            dma((2, 2, 8)),
            dma((2, 2, 8)),
            dma((4,)),
            dma((4,)),
            dma((2, 3)),
            dma((2, 3)),
            dma((8,)),
            dma((8,)),
            dma((8,)),
            dma((8,)),
        ],
        compiler_params=pltpu.CompilerParams(
            collective_id=0, has_side_effects=True, vmem_limit_bytes=56 * 1024 * 1024
        ),
    )(
        patches.reshape(ROWS, width),
        norm_gain.reshape(1, width),
        fc1_weight,
        fc2_weight,
        loc_bias,
        mine(layer_scale),
        mine(fc2_bias),
        target,
    )
    return received.reshape(NZ * NY * NX * 16, FEAT)


def solution(mesh):
    in_specs = (
        P("dp", None, None),
        P("dp"),
        P("dp", None),
        P(),
        P(),
        P("dp", "section"),
        P(),
        P("section", "dp"),
        P(),
        P(),
    )
    out_specs = P("dp", "section")
    return jax.shard_map(local, mesh=mesh, in_specs=in_specs, out_specs=out_specs, check_vma=False)
```

```python
import jax
import jax.numpy as jnp
from jax import lax
from jax.experimental import pallas as pl
from jax.experimental.pallas import tpu as pltpu
from jax.sharding import PartitionSpec as P

MESH = pl.DeviceIdType.MESH
F32 = jnp.float32
BF16 = jnp.bfloat16

NQ, NZ, NY, NX = 4, 2, 8, 4
D = 3200
FF = 800
FP = 896
SLOT = 200
SH = 50
SHP = 64
RUN = 200
RUNP = 208
FEAT = 400
ROWS = 512
TILES = 64
TOK = 256
Y_CUTS = ((0, 512), (512, 384))
X_CUTS = (
    ((0, 384), (384, 256), (640, 256)),
    ((0, 384), (384, 384), (768, 128)),
)


def md(a, n):
    return lax.rem(a, jnp.int32(n))


def dv(a, n):
    return lax.div(a, jnp.int32(n))


def dot(a, b, dims=((1,), (0,))):
    return lax.dot_general(a, b, (dims, ((), ())), preferred_element_type=F32)


def iota(shape, dim):
    return lax.broadcasted_iota(jnp.int32, shape, dim)


def window(start):
    block = dv(start, 128) - dv(start, 3000)
    return pl.multiple_of(block * 128, 128), start - block * 128


def kernel(
    patches_hbm,
    counts,
    owners,
    plan,
    gain,
    w1,
    bias1,
    w2t,
    bias2,
    scale2,
    out,
    patches,
    rows,
    own,
    stage,
    wall,
    normed,
    acc,
    loc_bias,
    hidden,
    part,
    pair,
    far,
    far_in,
    side,
    side_in,
    branch,
    encoded,
    going,
    coming,
    turned,
    l_sem,
    st_send,
    st_recv,
    y_send,
    y_recv,
    x_send,
    x_recv,
    c_send,
    c_recv,
    f_send,
    f_recv,
    s_send,
    s_recv,
    a_send,
    a_recv,
    b_send,
    b_recv,
):
    s = lax.axis_index("section")
    d = lax.axis_index("dp")
    q, c = dv(s, 2), md(s, 2)
    z, y, x = dv(d, 32), md(dv(d, 4), 8), md(d, 4)
    h = md(x + z, 2)
    e = md(x, 2)

    def dp_id(z_, y_, x_):
        return (s, z_ * 32 + y_ * 4 + x_)

    def peer(step):
        g = md(z * 4 + x + step, 8)
        return g, dv(g, 4), md(g, 4)

    def copy(src, dst, send, recv, device):
        return pltpu.make_async_remote_copy(
            src_ref=src,
            dst_ref=dst,
            send_sem=send,
            recv_sem=recv,
            device_id=device,
            device_id_type=MESH,
        )

    mate = (q * 2 + 1 - c, d)
    q_up = (md(q + 1, NQ) * 2 + c, d)
    q_dn = (md(q + NQ - 1, NQ) * 2 + c, d)

    load = pltpu.make_async_copy(patches_hbm, patches, l_sem)
    load.start()

    barrier = pltpu.get_barrier_semaphore()
    for step in range(1, 8):
        _, zp, xp = peer(step)
        for device in (dp_id(zp, y, xp), dp_id(z, md(y + step, 8), x)):
            pl.semaphore_signal(barrier, inc=1, device_id=device, device_id_type=MESH)
    for device in (mate, q_up, q_dn):
        pl.semaphore_signal(barrier, inc=1, device_id=device, device_id_type=MESH)

    own[...] = jnp.zeros_like(own)
    own[0, 0:SH, 0:FF] = w1[...]
    own[1, 0:SH, 0:FF] = w2t[...]

    pl.semaphore_wait(barrier, 17)

    def stage_copy(m, k, l):
        return copy(
            own.at[m],
            stage.at[m, x],
            st_send.at[m, 2 * k + l],
            st_recv.at[m, x],
            dp_id(md(z + l, 2), y, md(x + md(e + l, 2) + 2 * k, 4)),
        )

    def stage_start(m):
        for k in range(2):
            for l in range(2):
                if k or l:
                    stage_copy(m, k, l).start()
        pl.when(e == 1)(lambda: stage_copy(m, 0, 0).start())

        @pl.when(e == 0)
        def _():
            stage[m, x] = own[m]

    def stage_arrive(m, j):
        xs = md(x + j, 4)
        copy(own.at[m], stage.at[m, xs], st_send.at[m, 0], st_recv.at[m, xs], dp_id(z, y, x)).wait_recv()

    def stage_finish(m):
        pl.when(e == 1)(lambda: stage_arrive(m, 0))
        for j in range(1, 4):
            stage_arrive(m, j)
        row, col = iota((RUNP, 4 * SHP), 0), iota((RUNP, 4 * SHP), 1)
        pick = ((col == dv(row, SH) * SHP + md(row, SH)) & (row < RUN)).astype(BF16)
        wall[m, y, h] = dot(pick, stage[m].reshape(4 * SHP, FP)).astype(BF16)

    def y_copy(m, way, t, arriving=False):
        back = t + 1 if arriving else t
        b = md(y + 8 - back, 8) if way == 0 else md(y + back, 8)
        to = md(y + 1, 8) if way == 0 else md(y + 7, 8)
        start, size = (0, FP) if t < 3 else Y_CUTS[(way + m) % 2]
        ref = wall.at[m, b, h, :, pl.ds(start, size)]
        return copy(ref, ref, y_send.at[m, way, t], y_recv.at[m, way, t], dp_id(z, to, x))

    def x_copy(m, cut, b, arriving=False):
        to = dp_id(1 - z, y, x) if cut == 2 else dp_id(z, y, md(x + 1 + 2 * md(b + cut, 2), 4))
        half = 1 - h if arriving else h
        start, size = X_CUTS[m][cut]
        ref = wall.at[m, b, half, :, pl.ds(start, size)]
        return copy(ref, ref, x_send.at[m, cut, b], x_recv.at[m, cut, b], to)

    def block_at(way, t):
        return md(y + 8 - t, 8) if way == 0 else md(y + t, 8)

    def send_block(m, t):
        for way in range(2):
            if t > 0:
                y_copy(m, way, t - 1, True).wait_recv()
            if t < 4:
                y_copy(m, way, t).start()
            if t in (1, 2, 3):
                for cut in range(3):
                    x_copy(m, cut, block_at(way, t)).start()
        if t in (0, 4):
            for cut in range(3):
                x_copy(m, cut, block_at(0, t)).start()

    def each(t, use):
        def one(way, carry):
            use(md(y + way * t + (1 - way) * (8 - t), 8))
            return carry

        lax.fori_loop(0, 1 if t in (0, 4) else 2, one, 0)

    def x_arrive(m, b):
        for cut in range(3):
            x_copy(m, cut, b, True).wait_recv()

    def fc1(b):
        x_arrive(0, b)
        total = None
        for half in range(2):
            at, off = window(half * 1600 + b * RUN)
            row, col = iota((384, 2 * RUNP), 0), iota((384, 2 * RUNP), 1) - half * RUNP
            pick = ((row == col + off) & (col >= 0) & (col < RUN)).astype(BF16)
            term = dot(normed[:, pl.ds(at, 384)], pick)
            total = term if total is None else total + term
        acc[...] += dot(total.astype(BF16), wall[0, b].reshape(2 * RUNP, FP))

    def roles(b):
        rel = md(q + NQ - dv(b, 4), NQ)
        return c == md(dv(b, 2), 2), rel, dv(b, 4) * 2 + md(b, 2), md(b, 2)

    def pair_copy(b, slot):
        return copy(part.at[b], pair.at[slot], c_send.at[slot], c_recv.at[slot], mate)

    def far_copy(j, half):
        return copy(
            far.at[j, :, pl.ds(half * TOK, TOK)],
            far_in.at[j, half],
            f_send.at[j, half],
            f_recv.at[j, half],
            q_up if half else q_dn,
        )

    def side_copy(j, way):
        return copy(
            side.at[j, way], side_in.at[j, way], s_send.at[j, way], s_recv.at[j, way], q_up if way else q_dn
        )

    def fc2(b):
        x_arrive(1, b)
        term = dot(wall[1, b].reshape(2 * RUNP, FP), hidden[...], ((1,), (1,))).astype(BF16)
        part[b] = term.reshape(2, RUNP, ROWS)
        mine, _, slot, _ = roles(b)

        @pl.when(jnp.logical_not(mine))
        def _():
            pair_copy(b, slot).start()

    def both(b, slot, run):
        return part[b, run].astype(F32) + pair[slot, run].astype(F32)

    def sum_far(b):
        mine, rel, slot, j = roles(b)

        @pl.when(mine)
        def _():
            pair_copy(b, slot).wait_recv()

            @pl.when(md(rel, 2) == 0)
            def _():
                far[j] = both(b, slot, 1 - dv(rel, 2)).astype(BF16)
                for half in range(2):
                    far_copy(j, half).start()

    def sum_side(b):
        mine, rel, slot, j = roles(b)

        @pl.when(mine & (md(rel, 2) == 1))
        def _():
            for way in range(2):
                far_copy(j, way).wait_recv()
                run = dv(rel, 2) if way == 0 else 1 - dv(rel, 2)
                total = both(b, slot, run)
                lo, hi = total[:, 0:TOK], total[:, TOK:ROWS]
                if way == 0:
                    lo = lo + far_in[j, 0].astype(F32)
                else:
                    hi = hi + far_in[j, 1].astype(F32)
                side[j, way, :, 0:TOK] = lo.astype(BF16)
                side[j, way, :, TOK:ROWS] = hi.astype(BF16)
                side_copy(j, way).start()

    def sum_end(b):
        mine, rel, slot, j = roles(b)

        @pl.when(mine & (md(rel, 2) == 0))
        def _():
            for way in range(2):
                side_copy(j, way).wait_recv()
            total = both(b, slot, dv(rel, 2))
            branch[j] = total + side_in[j, 0].astype(F32) + side_in[j, 1].astype(F32)

    stage_start(0)
    stage_start(1)

    for i, ref in enumerate((gain, bias2, scale2)):
        rows[i : i + 1, :] = ref[...].reshape(1, D)

    stage_finish(0)
    send_block(0, 0)

    load.wait()

    def norm(i, carry):
        at = pl.ds(pl.multiple_of(i * 64, 64), 64)
        values = patches[at, :].astype(F32)
        scale = lax.rsqrt(jnp.mean(values * values, axis=1, keepdims=True) + 1e-06)
        normed[at, :] = (values * scale * rows[0:1, :]).astype(BF16)
        return carry

    lax.fori_loop(0, 8, norm, 0)
    acc[...] = jnp.zeros_like(acc)
    stage_finish(1)

    send_block(0, 1)
    each(0, fc1)
    send_block(0, 2)
    send_block(1, 0)
    each(1, fc1)

    loc_bias[...] = jnp.zeros_like(loc_bias)
    for k in range(4):
        held = jnp.zeros((1, SLOT), F32)
        for p in range(32):
            held = jnp.where(plan[k, s] == p, bias1[p * SLOT : (p + 1) * SLOT].reshape(1, SLOT), held)
        loc_bias[:, k * SLOT : (k + 1) * SLOT] = held

    send_block(0, 3)
    each(2, fc1)
    send_block(1, 1)
    send_block(0, 4)
    each(3, fc1)
    each(4, fc1)

    def gelu(i, carry):
        at = pl.ds(pl.multiple_of(i * 64, 64), 64)
        pre = acc[at, :] + loc_bias[...]
        hidden[at, :] = (0.5 * pre * (1.0 + lax.erf(pre * 0.7071067811865476))).astype(BF16)
        return carry

    lax.fori_loop(0, 8, gelu, 0)
    send_block(1, 2)
    each(0, fc2)
    each(1, fc2)
    each(0, sum_far)
    each(1, sum_far)

    owner_row = owners[...]
    eye = iota((TILES, TILES), 0) == iota((TILES, TILES), 1)
    owner = jnp.sum(jnp.where(eye, owner_row, 0).astype(F32), axis=1, keepdims=True).astype(jnp.int32)
    earlier = iota((TILES, TILES), 0) > iota((TILES, TILES), 1)
    rank = jnp.sum(((owner == owner_row) & earlier).astype(F32), axis=1, keepdims=True).astype(jnp.int32)
    tile = iota((TILES, 1), 0)
    count = jnp.zeros((TILES, 1), jnp.int32)
    for i in range(8):
        count = jnp.where(dv(tile, 8) == i, counts[i], count)
    place = md(dv(owner, 4), 8) * 128 + (dv(owner, 32) * 4 + md(owner, 4)) * 16 + rank * 8
    place = jnp.where(md(tile, 8) < count, place, -4096)
    token = iota((TILES, ROWS), 1)
    spread = jnp.where(iota((TILES, ROWS), 0) == dv(token, 8), place, 0).astype(F32)
    target = jnp.sum(spread, axis=0, keepdims=True).astype(jnp.int32) + md(iota((1, ROWS), 1), 8)

    send_block(1, 3)
    each(0, sum_side)
    each(2, fc2)
    each(2, sum_far)
    each(1, sum_side)
    send_block(1, 4)
    each(3, fc2)
    each(3, sum_far)
    each(0, sum_end)
    each(2, sum_side)
    each(4, fc2)
    each(4, sum_far)
    each(1, sum_end)
    each(3, sum_side)
    each(2, sum_end)
    each(4, sum_side)
    each(3, sum_end)
    each(4, sum_end)

    for j in range(2):
        at, off = window(s * FEAT + j * RUN)
        row, col = iota((RUNP, 384), 0), iota((RUNP, 384), 1)
        chosen = (col == row + off) & (row < RUN)
        values = dot(chosen.astype(BF16), patches[:, pl.ds(at, 384)], ((1,), (1,)))
        bias, scale = (
            jnp.sum(jnp.where(chosen, rows[i : i + 1, pl.ds(at, 384)], 0.0), axis=1, keepdims=True)
            for i in (1, 2)
        )
        encoded[j * RUNP : (j + 1) * RUNP] = (values + scale * (branch[j] + bias)).astype(BF16)

    def a_copy(step, arriving=False):
        to = md(y + step, 8)
        src = md(y + 8 - step, 8) if arriving else y
        return copy(going.at[to], coming.at[src], a_send.at[step], a_recv.at[step], dp_id(z, to, x))

    def put(step):
        to = md(y + step, 8)
        pick = (target == iota((128, ROWS), 0) + to * 128).astype(BF16)
        going[to] = dot(encoded[...], pick, ((1,), (1,))).astype(BF16)

    for step in (4, 3, 5, 2, 6, 1, 7):
        put(step)
        a_copy(step).start()
    put(0)

    row, col = iota((2 * RUNP, FEAT), 0), iota((2 * RUNP, FEAT), 1)
    keep = (row == col + jnp.where(col >= RUN, RUNP - RUN, 0)).astype(BF16)

    def b_copy(step, src, arriving=False):
        g, zp, xp = peer(8 - step) if arriving else peer(step)
        zo, xo = (zp, xp) if arriving else (z, x)
        return copy(
            turned.at[g, src], out.at[zo, src, xo], b_send.at[step, src], b_recv.at[step, src], dp_id(zp, y, xp)
        )

    def turn(src, block):
        turned[:, src] = dot(block, keep, ((0,), (0,))).astype(BF16).reshape(8, 16, FEAT)

        def send(step, carry):
            b_copy(step, src).start()
            return carry

        lax.fori_loop(1, 8, send, 0)

    turn(y, going[y])
    for step in (1, 7, 2, 6, 3, 5, 4):
        a_copy(step, True).wait_recv()
        src = md(y + 8 - step, 8)
        turn(src, coming[src])

    out[z, :, x] = turned[z * 4 + x]

    def finish(i, carry):
        step, src = dv(i, 8) + 1, md(i, 8)
        b_copy(step, src, True).wait_recv()
        b_copy(step, src).wait_send()
        return carry

    lax.fori_loop(0, 56, finish, 0)

    for m in range(2):
        for k in range(2):
            for l in range(2):
                if k or l:
                    stage_copy(m, k, l).wait_send()
        pl.when(e == 1)(lambda: stage_copy(m, 0, 0).wait_send())
        for way in range(2):
            for t in range(4):
                y_copy(m, way, t).wait_send()
        for cut in range(3):
            for b in range(8):
                x_copy(m, cut, b).wait_send()
    for slot in range(4):
        pair_copy(0, slot).wait_send()
    for j in range(2):
        for way in range(2):
            far_copy(j, way).wait_send()
            side_copy(j, way).wait_send()
    for step in range(1, 8):
        a_copy(step).wait_send()


def local(
    patches,
    tile_counts,
    owners,
    plan,
    norm_gain,
    fc1_weight,
    fc1_bias,
    fc2_weight,
    fc2_bias,
    layer_scale,
):
    width = patches.shape[2]
    vmem = pl.BlockSpec(memory_space=pltpu.VMEM)
    smem = pl.BlockSpec(memory_space=pltpu.SMEM)
    dma = pltpu.SemaphoreType.DMA
    received = pl.pallas_call(
        kernel,
        out_shape=jax.ShapeDtypeStruct((NZ, NY, NX, 16, FEAT), BF16),
        in_specs=[pl.BlockSpec(memory_space=pl.ANY), smem, vmem, smem] + [vmem] * 6,
        out_specs=vmem,
        scratch_shapes=[
            pltpu.VMEM((ROWS, D), BF16),
            pltpu.VMEM((8, D), F32),
            pltpu.VMEM((2, SHP, FP), BF16),
            pltpu.VMEM((2, 4, SHP, FP), BF16),
            pltpu.VMEM((2, 8, 2, RUNP, FP), BF16),
            pltpu.VMEM((ROWS, D), BF16),
            pltpu.VMEM((ROWS, FP), F32),
            pltpu.VMEM((1, FP), F32),
            pltpu.VMEM((ROWS, FP), BF16),
            pltpu.VMEM((8, 2, RUNP, ROWS), BF16),
            pltpu.VMEM((4, 2, RUNP, ROWS), BF16),
            pltpu.VMEM((2, RUNP, ROWS), BF16),
            pltpu.VMEM((2, 2, RUNP, TOK), BF16),
            pltpu.VMEM((2, 2, RUNP, ROWS), BF16),
            pltpu.VMEM((2, 2, RUNP, ROWS), BF16),
            pltpu.VMEM((2, RUNP, ROWS), F32),
            pltpu.VMEM((2 * RUNP, ROWS), BF16),
            pltpu.VMEM((8, 2 * RUNP, 128), BF16),
            pltpu.VMEM((8, 2 * RUNP, 128), BF16),
            pltpu.VMEM((8, 8, 16, FEAT), BF16),
            dma,
            dma((2, 4)),
            dma((2, 4)),
            dma((2, 2, 4)),
            dma((2, 2, 4)),
            dma((2, 3, 8)),
            dma((2, 3, 8)),
            dma((4,)),
            dma((4,)),
            dma((2, 2)),
            dma((2, 2)),
            dma((2, 2)),
            dma((2, 2)),
            dma((8,)),
            dma((8,)),
            dma((8, 8)),
            dma((8, 8)),
        ],
        compiler_params=pltpu.CompilerParams(
            collective_id=0, has_side_effects=True, vmem_limit_bytes=56 * 1024 * 1024
        ),
    )(
        patches.reshape(ROWS, width),
        tile_counts,
        owners.T,
        plan.T,
        norm_gain,
        fc1_weight,
        fc1_bias,
        fc2_weight.T,
        fc2_bias,
        layer_scale,
    )
    return received.reshape(NZ * NY * NX * 16, FEAT)


def solution(mesh):
    in_specs = (
        P("dp", None, None),
        P("dp"),
        P("dp", None),
        P(),
        P(),
        P("dp", "section"),
        P(),
        P("section", "dp"),
        P(),
        P(),
    )
    out_specs = P("dp", "section")
    return jax.shard_map(local, mesh=mesh, in_specs=in_specs, out_specs=out_specs, check_vma=False)
```

```python
import jax
import jax.numpy as jnp
from jax import lax
from jax.experimental import pallas as pl
from jax.experimental.pallas import tpu as pltpu
from jax.sharding import PartitionSpec as P

MESH = pl.DeviceIdType.MESH
F32 = jnp.float32
BF16 = jnp.bfloat16

NQ, NZ, NY, NX = 4, 2, 8, 4
D = 3200
FF = 800
FP = 896
SLOT = 200
SH = 50
SHP = 64
RUN = 200
RUNP = 208
FEAT = 400
ROWS = 512
TILES = 64
QUARTER = RUNP // 4
LAST = 6 * RUNP
PACKED = LAST + 64
HALF = PACKED // 2


def x_cuts(m, t):
    return ((0, 656), (656, 656)) if m == 1 and t > 1 else ((0, 432), (432, 432), (864, 448))


def md(a, n):
    return lax.rem(a, jnp.int32(n))


def dv(a, n):
    return lax.div(a, jnp.int32(n))


def dot(a, b, dims=((1,), (0,))):
    return lax.dot_general(a, b, (dims, ((), ())), preferred_element_type=F32)


def iota(shape, dim):
    return lax.broadcasted_iota(jnp.int32, shape, dim)


def window(start):
    block = dv(start, 128) - dv(start, 3000)
    return pl.multiple_of(block * 128, 128), start - block * 128


def kernel(
    patches_hbm,
    counts,
    owners,
    plan,
    gain,
    w1,
    bias1,
    w2t,
    bias2,
    scale2,
    out,
    patches,
    rows,
    own,
    stage,
    wall,
    flat,
    normed,
    acc,
    loc_bias,
    hidden,
    part,
    pair,
    far,
    side,
    sums_in,
    base,
    scales,
    picks,
    going,
    coming,
    turned,
    l_sem,
    st_send,
    st_recv,
    y_send,
    y_recv,
    x_send,
    x_recv,
    c_send,
    c_recv,
    s_send,
    s_recv,
    a_send,
    a_recv,
    b_send,
    b_recv,
):
    s = lax.axis_index("section")
    d = lax.axis_index("dp")
    q, c = dv(s, 2), md(s, 2)
    z, y, x = dv(d, 32), md(dv(d, 4), 8), md(d, 4)
    h = md(x + z, 2)
    e = md(x, 2)

    def dp_id(z_, y_, x_):
        return (s, z_ * 32 + y_ * 4 + x_)

    def peer(step):
        g = md(z * 4 + x + step, 8)
        return g, dv(g, 4), md(g, 4)

    def copy(src, dst, send, recv, device):
        return pltpu.make_async_remote_copy(
            src_ref=src,
            dst_ref=dst,
            send_sem=send,
            recv_sem=recv,
            device_id=device,
            device_id_type=MESH,
        )

    mate = (q * 2 + 1 - c, d)
    q_up = (md(q + 1, NQ) * 2 + c, d)
    q_dn = (md(q + NQ - 1, NQ) * 2 + c, d)
    q_far = (md(q + 2, NQ) * 2 + c, d)

    load = pltpu.make_async_copy(patches_hbm, patches, l_sem)
    load.start()

    barrier = pltpu.get_barrier_semaphore()
    for step in range(1, 8):
        _, zp, xp = peer(step)
        pl.semaphore_signal(barrier, inc=1, device_id=dp_id(zp, y, xp), device_id_type=MESH)
    for device in (dp_id(z, md(y + 1, 8), x), dp_id(z, md(y + 7, 8), x), mate, q_up, q_dn, q_far):
        pl.semaphore_signal(barrier, inc=1, device_id=device, device_id_type=MESH)

    own[...] = jnp.zeros_like(own)
    own[0, 0:SH, 0:FF] = w1[...]
    own[1, 0:SH, 0:FF] = w2t[...]

    pl.semaphore_wait(barrier, 13)

    quarters = dv(iota((RUNP, 128), 0), QUARTER) == dv(iota((RUNP, 128), 1), 32)

    def stage_copy(m, k, l):
        return copy(
            own.at[m],
            stage.at[m, x],
            st_send.at[m, 2 * k + l],
            st_recv.at[m, x],
            dp_id(md(z + l, 2), y, md(x + md(e + l, 2) + 2 * k, 4)),
        )

    def stage_start(m):
        for k in range(2):
            for l in range(2):
                if k or l:
                    stage_copy(m, k, l).start()
        pl.when(e == 1)(lambda: stage_copy(m, 0, 0).start())

        @pl.when(e == 0)
        def _():
            stage[m, x] = own[m]

    def stage_arrive(m, j):
        xs = md(x + j, 4)
        copy(own.at[m], stage.at[m, xs], st_send.at[m, 0], st_recv.at[m, xs], dp_id(z, y, x)).wait_recv()

    def stage_finish(m):
        pl.when(e == 1)(lambda: stage_arrive(m, 0))
        for j in range(1, 4):
            stage_arrive(m, j)
        row, col = iota((RUNP, 4 * SHP), 0), iota((RUNP, 4 * SHP), 1)
        pick = ((col == dv(row, SH) * SHP + md(row, SH)) & (row < RUN)).astype(BF16)
        whole = dot(pick, stage[m].reshape(4 * SHP, FP)).astype(BF16)
        for i in range(6):
            wall[m, y, h, i * RUNP : (i + 1) * RUNP, :] = whole[:, i * 128 : (i + 1) * 128]
        spread = (iota((128, 128), 0) == md(iota((128, 128), 1), 32)).astype(BF16)
        last = jnp.where(quarters, dot(whole[:, 768:FP], spread), 0.0).astype(BF16)
        fold = (iota((64, RUNP), 0) == md(iota((64, RUNP), 1), QUARTER)).astype(BF16)
        wall[m, y, h, LAST:PACKED, :] = dot(fold, last).astype(BF16)

    def unpack(m, b):
        for half in range(2):
            at = slice(half * RUNP, (half + 1) * RUNP)
            for i in range(6):
                flat[at, i * 128 : (i + 1) * 128] = wall[m, b, half, i * RUNP : (i + 1) * RUNP, :]
            unfold = (iota((RUNP, 64), 1) == md(iota((RUNP, 64), 0), QUARTER)).astype(BF16)
            last = jnp.where(quarters, dot(unfold, wall[m, b, half, LAST:PACKED, :]), 0.0).astype(BF16)
            gather = (md(iota((128, 128), 0), 32) == iota((128, 128), 1)).astype(BF16)
            flat[at, 768:FP] = dot(last, gather).astype(BF16)

    def y_copy(m, way, t, part, arriving=False):
        back = t + 1 if arriving else t
        b = md(y + 8 - back, 8) if way == 0 else md(y + back, 8)
        to = md(y + 1, 8) if way == 0 else md(y + 7, 8)
        ref = wall.at[m, b, h, pl.ds(part * HALF, HALF)]
        return copy(ref, ref, y_send.at[m, way, t, part], y_recv.at[m, way, t, part], dp_id(z, to, x))

    def x_copy(m, cut, b, t, arriving=False):
        to = (dp_id(z, y, md(x + 1, 4)), dp_id(z, y, md(x + 3, 4)), dp_id(1 - z, y, x))[cut]
        half = 1 - h if arriving else h
        start, size = x_cuts(m, t)[cut]
        ref = wall.at[m, b, half, pl.ds(start, size)]
        return copy(ref, ref, x_send.at[m, cut, b], x_recv.at[m, cut, b], to)

    def block_at(way, t):
        return md(y + 8 - t, 8) if way == 0 else md(y + t, 8)

    def y_parts(t):
        return [(way, part) for part in range(2) for way in range(2) if t < 3 or part == way]

    def send_y(m, t):
        if t == 0:
            for way, part in y_parts(0):
                y_copy(m, way, 0, part).start()
            return
        for way, part in y_parts(t - 1):
            y_copy(m, way, t - 1, part, True).wait_recv()
            if t < 4 and (way, part) in y_parts(t):
                y_copy(m, way, t, part).start()

    def send_x(m, t):
        for way in range(1 if t in (0, 4) else 2):
            for cut in range(len(x_cuts(m, t))):
                x_copy(m, cut, block_at(way, t), t).start()

    def send_block(m, t):
        send_y(m, t)
        send_x(m, t)

    def each(t, use):
        def one(way, carry):
            use(md(y + way * t + (1 - way) * (8 - t), 8), t)
            return carry

        lax.fori_loop(0, 1 if t in (0, 4) else 2, one, 0)

    def x_arrive(m, b, t):
        for cut in range(len(x_cuts(m, t))):
            x_copy(m, cut, b, t, True).wait_recv()

    def fc1(b, t):
        x_arrive(0, b, t)
        total = None
        for half in range(2):
            at, off = window(half * 1600 + b * RUN)
            row, col = iota((384, 2 * RUNP), 0), iota((384, 2 * RUNP), 1) - half * RUNP
            pick = ((row == col + off) & (col >= 0) & (col < RUN)).astype(BF16)
            term = dot(normed[:, pl.ds(at, 384)], pick)
            total = term if total is None else total + term
        unpack(0, b)
        acc[...] += dot(total.astype(BF16), flat[...])

    def roles(b):
        rel = md(q + NQ - dv(b, 4), NQ)
        return c == md(dv(b, 2), 2), rel, dv(b, 4) * 2 + md(b, 2), md(b, 2)

    def pair_copy(b, slot):
        return copy(part.at[b], pair.at[slot], c_send.at[slot], c_recv.at[slot], mate)

    def side_copy(j, way):
        to = q_up if way else q_dn
        return copy(side.at[j, way], sums_in.at[j, way], s_send.at[j, way], s_recv.at[j, way], to)

    def far_copy(j):
        return copy(far.at[j], sums_in.at[j, 2], s_send.at[j, 2], s_recv.at[j, 2], q_far)

    def fc2(b, t):
        x_arrive(1, b, t)
        unpack(1, b)
        term = dot(flat[...], hidden[...], ((1,), (1,))).astype(BF16)
        part[b] = term.reshape(2, RUNP, ROWS)
        mine, _, slot, _ = roles(b)

        @pl.when(jnp.logical_not(mine))
        def _():
            pair_copy(b, slot).start()

    def both(b, slot, run):
        return part[b, run].astype(F32) + pair[slot, run].astype(F32)

    def sum_send(b, t):
        mine, rel, slot, j = roles(b)

        @pl.when(mine)
        def _():
            pair_copy(b, slot).wait_recv()

            @pl.when(md(rel, 2) == 0)
            def _():
                far[j] = both(b, slot, 1 - dv(rel, 2)).astype(BF16)
                far_copy(j).start()

            @pl.when(md(rel, 2) == 1)
            def _():
                side[j, 0] = both(b, slot, dv(rel, 2)).astype(BF16)
                side_copy(j, 0).start()
                side[j, 1] = both(b, slot, 1 - dv(rel, 2)).astype(BF16)
                side_copy(j, 1).start()

    def sum_end(b, t):
        mine, rel, slot, j = roles(b)

        @pl.when(mine & (md(rel, 2) == 0))
        def _():
            total = both(b, slot, dv(rel, 2))
            for way in range(3):
                (far_copy(j) if way == 2 else side_copy(j, way)).wait_recv()
                total = total + sums_in[j, way].astype(F32)
            encoded = (base[j] + scales[j] * total).astype(BF16)
            for step in (4, 3, 5, 2, 6, 1, 7, 0):
                to = md(y + step, 8)
                going[j, to] = dot(encoded, picks[to], ((1,), (1,))).astype(BF16)
                if step:
                    a_copy(j, step).start()

    def a_copy(j, step, arriving=False):
        to = md(y + step, 8)
        src = md(y + 8 - step, 8) if arriving else y
        return copy(
            going.at[j, to], coming.at[j, src], a_send.at[j, step], a_recv.at[j, step], dp_id(z, to, x)
        )

    stage_start(0)

    for i, ref in enumerate((gain, bias2, scale2)):
        rows[i : i + 1, :] = ref[...].reshape(1, D)

    stage_finish(0)
    send_block(0, 0)
    stage_start(1)

    load.wait()

    def norm(i, carry):
        at = pl.ds(pl.multiple_of(i * 64, 64), 64)
        values = patches[at, :].astype(F32)
        scale = lax.rsqrt(jnp.mean(values * values, axis=1, keepdims=True) + 1e-06)
        normed[at, :] = (values * scale * rows[0:1, :]).astype(BF16)
        return carry

    lax.fori_loop(0, 8, norm, 0)
    acc[...] = jnp.zeros_like(acc)

    send_block(0, 1)
    each(0, fc1)
    stage_finish(1)

    loc_bias[...] = jnp.zeros_like(loc_bias)
    for k in range(4):
        held = jnp.zeros((1, SLOT), F32)
        for p in range(32):
            held = jnp.where(plan[k, s] == p, bias1[p * SLOT : (p + 1) * SLOT].reshape(1, SLOT), held)
        loc_bias[:, k * SLOT : (k + 1) * SLOT] = held

    send_block(0, 2)
    each(1, fc1)

    owner_row = owners[...]
    eye = iota((TILES, TILES), 0) == iota((TILES, TILES), 1)
    owner = jnp.sum(jnp.where(eye, owner_row, 0).astype(F32), axis=1, keepdims=True).astype(jnp.int32)
    earlier = iota((TILES, TILES), 0) > iota((TILES, TILES), 1)
    rank = jnp.sum(((owner == owner_row) & earlier).astype(F32), axis=1, keepdims=True).astype(jnp.int32)
    tile = iota((TILES, 1), 0)
    count = jnp.zeros((TILES, 1), jnp.int32)
    for i in range(8):
        count = jnp.where(dv(tile, 8) == i, counts[i], count)
    place = md(dv(owner, 4), 8) * 128 + (dv(owner, 32) * 4 + md(owner, 4)) * 16 + rank * 8
    place = jnp.where(md(tile, 8) < count, place, -4096)
    token = iota((TILES, ROWS), 1)
    spread = jnp.where(iota((TILES, ROWS), 0) == dv(token, 8), place, 0).astype(F32)
    target = jnp.sum(spread, axis=0, keepdims=True).astype(jnp.int32) + md(iota((1, ROWS), 1), 8)
    for to in range(8):
        picks[to] = (target == iota((128, ROWS), 0) + to * 128).astype(BF16)

    send_block(0, 3)
    send_y(1, 0)
    each(2, fc1)

    for j in range(2):
        at, off = window(s * FEAT + j * RUN)
        row, col = iota((RUNP, 384), 0), iota((RUNP, 384), 1)
        chosen = (col == row + off) & (row < RUN)
        values = dot(chosen.astype(BF16), patches[:, pl.ds(at, 384)], ((1,), (1,)))
        bias, scale = (
            jnp.sum(jnp.where(chosen, rows[i : i + 1, pl.ds(at, 384)], 0.0), axis=1, keepdims=True)
            for i in (1, 2)
        )
        base[j] = values + scale * bias
        scales[j] = scale

    send_block(0, 4)
    send_x(1, 0)
    each(3, fc1)
    each(4, fc1)
    send_block(1, 1)

    def gelu(i, carry):
        at = pl.ds(pl.multiple_of(i * 64, 64), 64)
        pre = acc[at, :] + loc_bias[...]
        hidden[at, :] = (0.5 * pre * (1.0 + lax.erf(pre * 0.7071067811865476))).astype(BF16)
        return carry

    lax.fori_loop(0, 8, gelu, 0)
    send_block(1, 2)
    each(0, fc2)
    each(1, fc2)
    each(0, sum_send)
    each(1, sum_send)
    send_block(1, 3)
    each(2, fc2)
    each(2, sum_send)
    send_block(1, 4)
    each(3, fc2)
    each(3, sum_send)
    each(4, fc2)
    each(4, sum_send)
    for t in range(5):
        each(t, sum_end)

    def b_copy(step, src, arriving=False):
        g, zp, xp = peer(8 - step) if arriving else peer(step)
        zo, xo = (zp, xp) if arriving else (z, x)
        return copy(
            turned.at[g, src], out.at[zo, src, xo], b_send.at[step, src], b_recv.at[step, src], dp_id(zp, y, xp)
        )

    def turn(src, held):
        block = None
        for j in range(2):
            keep = (iota((RUNP, FEAT), 1) == iota((RUNP, FEAT), 0) + j * RUN) & (iota((RUNP, FEAT), 0) < RUN)
            term = dot(held[j, src], keep.astype(BF16), ((0,), (0,)))
            block = term if block is None else block + term
        turned[:, src] = block.astype(BF16).reshape(8, 16, FEAT)

        def send(step, carry):
            b_copy(step, src).start()
            return carry

        lax.fori_loop(1, 8, send, 0)

    turn(y, going)
    for step in (1, 7, 2, 6, 3, 5, 4):
        for j in range(2):
            a_copy(j, step, True).wait_recv()
        turn(md(y + 8 - step, 8), coming)

    out[z, :, x] = turned[z * 4 + x]

    def finish(i, carry):
        step, src = dv(i, 8) + 1, md(i, 8)
        b_copy(step, src, True).wait_recv()
        b_copy(step, src).wait_send()
        return carry

    lax.fori_loop(0, 56, finish, 0)

    for m in range(2):
        for k in range(2):
            for l in range(2):
                if k or l:
                    stage_copy(m, k, l).wait_send()
        pl.when(e == 1)(lambda: stage_copy(m, 0, 0).wait_send())
        for t in range(4):
            for way, piece in y_parts(t):
                y_copy(m, way, t, piece).wait_send()
        for t in range(5):
            for way in range(1 if t in (0, 4) else 2):
                for cut in range(len(x_cuts(m, t))):
                    x_copy(m, cut, block_at(way, t), t).wait_send()
    for slot in range(4):
        pair_copy(0, slot).wait_send()
    for j in range(2):
        for way in range(2):
            side_copy(j, way).wait_send()
        far_copy(j).wait_send()
        for step in range(1, 8):
            a_copy(j, step).wait_send()


def local(
    patches,
    tile_counts,
    owners,
    plan,
    norm_gain,
    fc1_weight,
    fc1_bias,
    fc2_weight,
    fc2_bias,
    layer_scale,
):
    width = patches.shape[2]
    vmem = pl.BlockSpec(memory_space=pltpu.VMEM)
    smem = pl.BlockSpec(memory_space=pltpu.SMEM)
    dma = pltpu.SemaphoreType.DMA
    received = pl.pallas_call(
        kernel,
        out_shape=jax.ShapeDtypeStruct((NZ, NY, NX, 16, FEAT), BF16),
        in_specs=[pl.BlockSpec(memory_space=pl.ANY), smem, vmem, smem] + [vmem] * 6,
        out_specs=vmem,
        scratch_shapes=[
            pltpu.VMEM((ROWS, D), BF16),
            pltpu.VMEM((8, D), F32),
            pltpu.VMEM((2, SHP, FP), BF16),
            pltpu.VMEM((2, 4, SHP, FP), BF16),
            pltpu.VMEM((2, 8, 2, PACKED, 128), BF16),
            pltpu.VMEM((2 * RUNP, FP), BF16),
            pltpu.VMEM((ROWS, D), BF16),
            pltpu.VMEM((ROWS, FP), F32),
            pltpu.VMEM((1, FP), F32),
            pltpu.VMEM((ROWS, FP), BF16),
            pltpu.VMEM((8, 2, RUNP, ROWS), BF16),
            pltpu.VMEM((4, 2, RUNP, ROWS), BF16),
            pltpu.VMEM((2, RUNP, ROWS), BF16),
            pltpu.VMEM((2, 2, RUNP, ROWS), BF16),
            pltpu.VMEM((2, 3, RUNP, ROWS), BF16),
            pltpu.VMEM((2, RUNP, ROWS), F32),
            pltpu.VMEM((2, RUNP, 1), F32),
            pltpu.VMEM((8, 128, ROWS), BF16),
            pltpu.VMEM((2, 8, RUNP, 128), BF16),
            pltpu.VMEM((2, 8, RUNP, 128), BF16),
            pltpu.VMEM((8, 8, 16, FEAT), BF16),
            dma,
            dma((2, 4)),
            dma((2, 4)),
            dma((2, 2, 4, 2)),
            dma((2, 2, 4, 2)),
            dma((2, 3, 8)),
            dma((2, 3, 8)),
            dma((4,)),
            dma((4,)),
            dma((2, 3)),
            dma((2, 3)),
            dma((2, 8)),
            dma((2, 8)),
            dma((8, 8)),
            dma((8, 8)),
        ],
        compiler_params=pltpu.CompilerParams(
            collective_id=0, has_side_effects=True, vmem_limit_bytes=56 * 1024 * 1024
        ),
    )(
        patches.reshape(ROWS, width),
        tile_counts,
        owners.T,
        plan.T,
        norm_gain,
        fc1_weight,
        fc1_bias,
        fc2_weight.T,
        fc2_bias,
        layer_scale,
    )
    return received.reshape(NZ * NY * NX * 16, FEAT)


def solution(mesh):
    in_specs = (
        P("dp", None, None),
        P("dp"),
        P("dp", None),
        P(),
        P(),
        P("dp", "section"),
        P(),
        P("section", "dp"),
        P(),
        P(),
    )
    out_specs = P("dp", "section")
    return jax.shard_map(local, mesh=mesh, in_specs=in_specs, out_specs=out_specs, check_vma=False)
```

```python
import jax
import jax.numpy as jnp
from jax import lax
from jax.experimental import pallas as pl
from jax.experimental.pallas import tpu as pltpu
from jax.sharding import PartitionSpec as P

MESH = pl.DeviceIdType.MESH
F32 = jnp.float32
BF16 = jnp.bfloat16

NQ, NZ, NY, NX = 4, 2, 8, 4
D = 3200
FF = 800
FP = 896
SLOT = 200
SH = 50
SHP = 64
RUN = 200
RUNP = 208
FEAT = 400
ROWS = 512
TILES = 64
QUARTER = RUNP // 4
LAST = 6 * RUNP
PACKED = LAST + 64
HALF = PACKED // 2


def by_part(m, t):
    return m == 1 and t > 1


def x_cuts(m, t):
    return ((0, HALF), (HALF, HALF)) if by_part(m, t) else ((0, 432), (432, 432), (864, 448))


def md(a, n):
    return lax.rem(a, jnp.int32(n))


def dv(a, n):
    return lax.div(a, jnp.int32(n))


def dot(a, b, dims=((1,), (0,))):
    return lax.dot_general(a, b, (dims, ((), ())), preferred_element_type=F32)


def iota(shape, dim):
    return lax.broadcasted_iota(jnp.int32, shape, dim)


def window(start):
    block = dv(start, 128) - dv(start, 3000)
    return pl.multiple_of(block * 128, 128), start - block * 128


def kernel(
    patches_hbm,
    counts,
    owners,
    plan,
    gain,
    w1,
    bias1,
    w2t,
    bias2,
    scale2,
    out,
    patches,
    rows,
    own,
    stage,
    wall,
    flat,
    normed,
    acc,
    loc_bias,
    hidden,
    part,
    pair,
    far,
    side,
    sums_in,
    base,
    scales,
    picks,
    going,
    coming,
    turned,
    l_sem,
    st_send,
    st_recv,
    y_send,
    y_recv,
    x_send,
    x_recv,
    c_send,
    c_recv,
    s_send,
    s_recv,
    a_send,
    a_recv,
    b_send,
    b_recv,
):
    s = lax.axis_index("section")
    d = lax.axis_index("dp")
    q, c = dv(s, 2), md(s, 2)
    z, y, x = dv(d, 32), md(dv(d, 4), 8), md(d, 4)
    h = md(x + z, 2)
    e = md(x, 2)

    def dp_id(z_, y_, x_):
        return (s, z_ * 32 + y_ * 4 + x_)

    def peer(step):
        g = md(z * 4 + x + step, 8)
        return g, dv(g, 4), md(g, 4)

    def copy(src, dst, send, recv, device):
        return pltpu.make_async_remote_copy(
            src_ref=src,
            dst_ref=dst,
            send_sem=send,
            recv_sem=recv,
            device_id=device,
            device_id_type=MESH,
        )

    mate = (q * 2 + 1 - c, d)
    q_up = (md(q + 1, NQ) * 2 + c, d)
    q_dn = (md(q + NQ - 1, NQ) * 2 + c, d)
    q_far = (md(q + 2, NQ) * 2 + c, d)

    load = pltpu.make_async_copy(patches_hbm, patches, l_sem)
    load.start()

    barrier = pltpu.get_barrier_semaphore()
    for step in range(1, 8):
        _, zp, xp = peer(step)
        pl.semaphore_signal(barrier, inc=1, device_id=dp_id(zp, y, xp), device_id_type=MESH)
    for device in (dp_id(z, md(y + 1, 8), x), dp_id(z, md(y + 7, 8), x), mate, q_up, q_dn, q_far):
        pl.semaphore_signal(barrier, inc=1, device_id=device, device_id_type=MESH)

    own[...] = jnp.zeros_like(own)
    own[0, 0:SH, 0:FF] = w1[...]
    own[1, 0:SH, 0:FF] = w2t[...]

    pl.semaphore_wait(barrier, 13)

    quarters = dv(iota((RUNP, 128), 0), QUARTER) == dv(iota((RUNP, 128), 1), 32)

    def stage_copy(m, k, l):
        return copy(
            own.at[m],
            stage.at[m, x],
            st_send.at[m, 2 * k + l],
            st_recv.at[m, x],
            dp_id(md(z + l, 2), y, md(x + md(e + l, 2) + 2 * k, 4)),
        )

    def stage_start(m):
        for k in range(2):
            for l in range(2):
                if k or l:
                    stage_copy(m, k, l).start()
        pl.when(e == 1)(lambda: stage_copy(m, 0, 0).start())

        @pl.when(e == 0)
        def _():
            stage[m, x] = own[m]

    def stage_arrive(m, j):
        xs = md(x + j, 4)
        copy(own.at[m], stage.at[m, xs], st_send.at[m, 0], st_recv.at[m, xs], dp_id(z, y, x)).wait_recv()

    def stage_finish(m):
        pl.when(e == 1)(lambda: stage_arrive(m, 0))
        for j in range(1, 4):
            stage_arrive(m, j)
        row, col = iota((RUNP, 4 * SHP), 0), iota((RUNP, 4 * SHP), 1)
        pick = ((col == dv(row, SH) * SHP + md(row, SH)) & (row < RUN)).astype(BF16)
        whole = dot(pick, stage[m].reshape(4 * SHP, FP)).astype(BF16)
        for i in range(6):
            wall[m, y, h, i * RUNP : (i + 1) * RUNP, :] = whole[:, i * 128 : (i + 1) * 128]
        spread = (iota((128, 128), 0) == md(iota((128, 128), 1), 32)).astype(BF16)
        last = jnp.where(quarters, dot(whole[:, 768:FP], spread), 0.0).astype(BF16)
        fold = (iota((64, RUNP), 0) == md(iota((64, RUNP), 1), QUARTER)).astype(BF16)
        wall[m, y, h, LAST:PACKED, :] = dot(fold, last).astype(BF16)

    def unpack(m, b):
        for half in range(2):
            at = slice(half * RUNP, (half + 1) * RUNP)
            for i in range(6):
                flat[at, i * 128 : (i + 1) * 128] = wall[m, b, half, i * RUNP : (i + 1) * RUNP, :]
            unfold = (iota((RUNP, 64), 1) == md(iota((RUNP, 64), 0), QUARTER)).astype(BF16)
            last = jnp.where(quarters, dot(unfold, wall[m, b, half, LAST:PACKED, :]), 0.0).astype(BF16)
            gather = (md(iota((128, 128), 0), 32) == iota((128, 128), 1)).astype(BF16)
            flat[at, 768:FP] = dot(last, gather).astype(BF16)

    def y_copy(m, way, t, part, arriving=False):
        back = t + 1 if arriving else t
        b = md(y + 8 - back, 8) if way == 0 else md(y + back, 8)
        to = md(y + 1, 8) if way == 0 else md(y + 7, 8)
        ref = wall.at[m, b, h, pl.ds(part * HALF, HALF)]
        return copy(ref, ref, y_send.at[m, way, t, part], y_recv.at[m, way, t, part], dp_id(z, to, x))

    def x_copy(m, cut, b, t, arriving=False):
        to = (dp_id(z, y, md(x + 1, 4)), dp_id(z, y, md(x + 3, 4)), dp_id(1 - z, y, x))[cut]
        half = 1 - h if arriving else h
        start, size = x_cuts(m, t)[cut]
        ref = wall.at[m, b, half, pl.ds(start, size)]
        return copy(ref, ref, x_send.at[m, cut, b], x_recv.at[m, cut, b], to)

    def block_at(way, t):
        return md(y + 8 - t, 8) if way == 0 else md(y + t, 8)

    def y_parts(t):
        return [(way, part) for part in range(2) for way in range(2) if t < 3 or part == way]

    def send_y(m, t):
        if t == 0:
            for way, part in y_parts(0):
                y_copy(m, way, 0, part).start()
            return
        for way, part in y_parts(t - 1):
            y_copy(m, way, t - 1, part, True).wait_recv()
            if t < 4 and (way, part) in y_parts(t):
                y_copy(m, way, t, part).start()
            if by_part(m, t):
                x_copy(m, part, block_at(way, t), t).start()

    def send_x(m, t):
        for way in range(1 if t in (0, 4) else 2):
            for cut in range(len(x_cuts(m, t))):
                x_copy(m, cut, block_at(way, t), t).start()

    def send_block(m, t):
        send_y(m, t)
        if not by_part(m, t):
            send_x(m, t)

    def each(t, use):
        def one(way, carry):
            use(md(y + way * t + (1 - way) * (8 - t), 8), t)
            return carry

        lax.fori_loop(0, 1 if t in (0, 4) else 2, one, 0)

    def x_arrive(m, b, t):
        for cut in range(len(x_cuts(m, t))):
            x_copy(m, cut, b, t, True).wait_recv()

    def fc1(b, t):
        x_arrive(0, b, t)
        total = None
        for half in range(2):
            at, off = window(half * 1600 + b * RUN)
            row, col = iota((384, 2 * RUNP), 0), iota((384, 2 * RUNP), 1) - half * RUNP
            pick = ((row == col + off) & (col >= 0) & (col < RUN)).astype(BF16)
            term = dot(normed[:, pl.ds(at, 384)], pick)
            total = term if total is None else total + term
        unpack(0, b)
        acc[...] += dot(total.astype(BF16), flat[...])

    def roles(b):
        rel = md(q + NQ - dv(b, 4), NQ)
        return c == md(dv(b, 2), 2), rel, dv(b, 4) * 2 + md(b, 2), md(b, 2)

    def pair_copy(b, slot):
        return copy(part.at[b], pair.at[slot], c_send.at[slot], c_recv.at[slot], mate)

    def side_copy(j, way):
        to = q_up if way else q_dn
        return copy(side.at[j, way], sums_in.at[j, way], s_send.at[j, way], s_recv.at[j, way], to)

    def far_copy(j):
        return copy(far.at[j], sums_in.at[j, 2], s_send.at[j, 2], s_recv.at[j, 2], q_far)

    def fc2(b, t):
        x_arrive(1, b, t)
        unpack(1, b)
        term = dot(flat[...], hidden[...], ((1,), (1,))).astype(BF16)
        part[b] = term.reshape(2, RUNP, ROWS)
        mine, _, slot, _ = roles(b)

        @pl.when(jnp.logical_not(mine))
        def _():
            pair_copy(b, slot).start()

    def both(b, slot, run):
        return part[b, run].astype(F32) + pair[slot, run].astype(F32)

    def sum_send(b, t):
        mine, rel, slot, j = roles(b)

        @pl.when(mine)
        def _():
            pair_copy(b, slot).wait_recv()

            @pl.when(md(rel, 2) == 0)
            def _():
                far[j] = both(b, slot, 1 - dv(rel, 2)).astype(BF16)
                far_copy(j).start()

            @pl.when(md(rel, 2) == 1)
            def _():
                side[j, 0] = both(b, slot, dv(rel, 2)).astype(BF16)
                side_copy(j, 0).start()
                side[j, 1] = both(b, slot, 1 - dv(rel, 2)).astype(BF16)
                side_copy(j, 1).start()

    def sum_end(b, t):
        mine, rel, slot, j = roles(b)

        @pl.when(mine & (md(rel, 2) == 0))
        def _():
            total = both(b, slot, dv(rel, 2))
            for way in range(3):
                (far_copy(j) if way == 2 else side_copy(j, way)).wait_recv()
                total = total + sums_in[j, way].astype(F32)
            encoded = (base[j] + scales[j] * total).astype(BF16)
            for step in (4, 3, 5, 2, 6, 1, 7, 0):
                to = md(y + step, 8)
                placed = dot(encoded, picks[to], ((1,), (1,))).astype(BF16)
                if step:
                    going[j, to] = placed
                    a_copy(j, step).start()
                else:
                    coming[j, y] = placed

    def a_copy(j, step, arriving=False):
        to = md(y + step, 8)
        src = md(y + 8 - step, 8) if arriving else y
        return copy(
            going.at[j, to], coming.at[j, src], a_send.at[j, step], a_recv.at[j, step], dp_id(z, to, x)
        )

    stage_start(0)

    for i, ref in enumerate((gain, bias2, scale2)):
        rows[i : i + 1, :] = ref[...].reshape(1, D)

    stage_finish(0)
    send_block(0, 0)
    stage_start(1)

    load.wait()

    def norm(i, carry):
        at = pl.ds(pl.multiple_of(i * 64, 64), 64)
        values = patches[at, :].astype(F32)
        scale = lax.rsqrt(jnp.mean(values * values, axis=1, keepdims=True) + 1e-06)
        normed[at, :] = (values * scale * rows[0:1, :]).astype(BF16)
        return carry

    lax.fori_loop(0, 8, norm, 0)
    acc[...] = jnp.zeros_like(acc)

    send_block(0, 1)
    each(0, fc1)
    stage_finish(1)

    loc_bias[...] = jnp.zeros_like(loc_bias)
    for k in range(4):
        held = jnp.zeros((1, SLOT), F32)
        for p in range(32):
            held = jnp.where(plan[k, s] == p, bias1[p * SLOT : (p + 1) * SLOT].reshape(1, SLOT), held)
        loc_bias[:, k * SLOT : (k + 1) * SLOT] = held

    send_block(0, 2)
    each(1, fc1)

    owner_row = owners[...]
    eye = iota((TILES, TILES), 0) == iota((TILES, TILES), 1)
    owner = jnp.sum(jnp.where(eye, owner_row, 0).astype(F32), axis=1, keepdims=True).astype(jnp.int32)
    earlier = iota((TILES, TILES), 0) > iota((TILES, TILES), 1)
    rank = jnp.sum(((owner == owner_row) & earlier).astype(F32), axis=1, keepdims=True).astype(jnp.int32)
    tile = iota((TILES, 1), 0)
    count = jnp.zeros((TILES, 1), jnp.int32)
    for i in range(8):
        count = jnp.where(dv(tile, 8) == i, counts[i], count)
    place = md(dv(owner, 4), 8) * 128 + (dv(owner, 32) * 4 + md(owner, 4)) * 16 + rank * 8
    place = jnp.where(md(tile, 8) < count, place, -4096)
    token = iota((TILES, ROWS), 1)
    spread = jnp.where(iota((TILES, ROWS), 0) == dv(token, 8), place, 0).astype(F32)
    target = jnp.sum(spread, axis=0, keepdims=True).astype(jnp.int32) + md(iota((1, ROWS), 1), 8)
    for to in range(8):
        picks[to] = (target == iota((128, ROWS), 0) + to * 128).astype(BF16)

    send_block(0, 3)
    send_y(1, 0)
    each(2, fc1)

    for j in range(2):
        at, off = window(s * FEAT + j * RUN)
        row, col = iota((RUNP, 384), 0), iota((RUNP, 384), 1)
        chosen = (col == row + off) & (row < RUN)
        values = dot(chosen.astype(BF16), patches[:, pl.ds(at, 384)], ((1,), (1,)))
        bias, scale = (
            jnp.sum(jnp.where(chosen, rows[i : i + 1, pl.ds(at, 384)], 0.0), axis=1, keepdims=True)
            for i in (1, 2)
        )
        base[j] = values + scale * bias
        scales[j] = scale

    send_block(0, 4)
    send_x(1, 0)
    each(3, fc1)
    each(4, fc1)
    send_block(1, 1)

    def gelu(i, carry):
        at = pl.ds(pl.multiple_of(i * 64, 64), 64)
        pre = acc[at, :] + loc_bias[...]
        hidden[at, :] = (0.5 * pre * (1.0 + lax.erf(pre * 0.7071067811865476))).astype(BF16)
        return carry

    lax.fori_loop(0, 8, gelu, 0)
    send_block(1, 2)
    each(0, fc2)
    each(1, fc2)
    each(0, sum_send)
    each(1, sum_send)
    send_block(1, 3)
    each(2, fc2)
    each(2, sum_send)
    send_block(1, 4)
    each(0, sum_end)
    each(1, sum_end)
    each(3, fc2)
    each(3, sum_send)
    each(4, fc2)
    each(4, sum_send)
    each(2, sum_end)
    each(3, sum_end)
    each(4, sum_end)

    def b_copy(step, src, arriving=False):
        g, zp, xp = peer(8 - step) if arriving else peer(step)
        zo, xo = (zp, xp) if arriving else (z, x)
        return copy(
            turned.at[g, src], out.at[zo, src, xo], b_send.at[step, src], b_recv.at[step, src], dp_id(zp, y, xp)
        )

    def turn(i, carry):
        odd = md(i, 2)
        src = md(2 * md(s, 4) + odd * dv(i + 1, 2) + (1 - odd) * (8 - dv(i, 2)), 8)
        step = md(y + 8 - src, 8)

        @pl.when(step > 0)
        def _():
            for j in range(2):
                a_copy(j, step, True).wait_recv()

        block = None
        for j in range(2):
            keep = (iota((RUNP, FEAT), 1) == iota((RUNP, FEAT), 0) + j * RUN) & (iota((RUNP, FEAT), 0) < RUN)
            term = dot(coming[j, src], keep.astype(BF16), ((0,), (0,)))
            block = term if block is None else block + term
        turned[:, src] = block.astype(BF16).reshape(8, 16, FEAT)

        def send(step, carry):
            b_copy(step, src).start()
            return carry

        return lax.fori_loop(1, 8, send, carry)

    lax.fori_loop(0, 8, turn, 0)

    out[z, :, x] = turned[z * 4 + x]

    def finish(i, carry):
        step, src = dv(i, 8) + 1, md(i, 8)
        b_copy(step, src, True).wait_recv()
        b_copy(step, src).wait_send()
        return carry

    lax.fori_loop(0, 56, finish, 0)

    for m in range(2):
        for k in range(2):
            for l in range(2):
                if k or l:
                    stage_copy(m, k, l).wait_send()
        pl.when(e == 1)(lambda: stage_copy(m, 0, 0).wait_send())
        for t in range(4):
            for way, piece in y_parts(t):
                y_copy(m, way, t, piece).wait_send()
        for t in range(5):
            for way in range(1 if t in (0, 4) else 2):
                for cut in range(len(x_cuts(m, t))):
                    x_copy(m, cut, block_at(way, t), t).wait_send()
    for slot in range(4):
        pair_copy(0, slot).wait_send()
    for j in range(2):
        for way in range(2):
            side_copy(j, way).wait_send()
        far_copy(j).wait_send()
        for step in range(1, 8):
            a_copy(j, step).wait_send()


def local(
    patches,
    tile_counts,
    owners,
    plan,
    norm_gain,
    fc1_weight,
    fc1_bias,
    fc2_weight,
    fc2_bias,
    layer_scale,
):
    width = patches.shape[2]
    vmem = pl.BlockSpec(memory_space=pltpu.VMEM)
    smem = pl.BlockSpec(memory_space=pltpu.SMEM)
    dma = pltpu.SemaphoreType.DMA
    received = pl.pallas_call(
        kernel,
        out_shape=jax.ShapeDtypeStruct((NZ, NY, NX, 16, FEAT), BF16),
        in_specs=[pl.BlockSpec(memory_space=pl.ANY), smem, vmem, smem] + [vmem] * 6,
        out_specs=vmem,
        scratch_shapes=[
            pltpu.VMEM((ROWS, D), BF16),
            pltpu.VMEM((8, D), F32),
            pltpu.VMEM((2, SHP, FP), BF16),
            pltpu.VMEM((2, 4, SHP, FP), BF16),
            pltpu.VMEM((2, 8, 2, PACKED, 128), BF16),
            pltpu.VMEM((2 * RUNP, FP), BF16),
            pltpu.VMEM((ROWS, D), BF16),
            pltpu.VMEM((ROWS, FP), F32),
            pltpu.VMEM((1, FP), F32),
            pltpu.VMEM((ROWS, FP), BF16),
            pltpu.VMEM((8, 2, RUNP, ROWS), BF16),
            pltpu.VMEM((4, 2, RUNP, ROWS), BF16),
            pltpu.VMEM((2, RUNP, ROWS), BF16),
            pltpu.VMEM((2, 2, RUNP, ROWS), BF16),
            pltpu.VMEM((2, 3, RUNP, ROWS), BF16),
            pltpu.VMEM((2, RUNP, ROWS), F32),
            pltpu.VMEM((2, RUNP, 1), F32),
            pltpu.VMEM((8, 128, ROWS), BF16),
            pltpu.VMEM((2, 8, RUNP, 128), BF16),
            pltpu.VMEM((2, 8, RUNP, 128), BF16),
            pltpu.VMEM((8, 8, 16, FEAT), BF16),
            dma,
            dma((2, 4)),
            dma((2, 4)),
            dma((2, 2, 4, 2)),
            dma((2, 2, 4, 2)),
            dma((2, 3, 8)),
            dma((2, 3, 8)),
            dma((4,)),
            dma((4,)),
            dma((2, 3)),
            dma((2, 3)),
            dma((2, 8)),
            dma((2, 8)),
            dma((8, 8)),
            dma((8, 8)),
        ],
        compiler_params=pltpu.CompilerParams(
            collective_id=0, has_side_effects=True, vmem_limit_bytes=56 * 1024 * 1024
        ),
    )(
        patches.reshape(ROWS, width),
        tile_counts,
        owners.T,
        plan.T,
        norm_gain,
        fc1_weight,
        fc1_bias,
        fc2_weight.T,
        fc2_bias,
        layer_scale,
    )
    return received.reshape(NZ * NY * NX * 16, FEAT)


def solution(mesh):
    in_specs = (
        P("dp", None, None),
        P("dp"),
        P("dp", None),
        P(),
        P(),
        P("dp", "section"),
        P(),
        P("section", "dp"),
        P(),
        P(),
    )
    out_specs = P("dp", "section")
    return jax.shard_map(local, mesh=mesh, in_specs=in_specs, out_specs=out_specs, check_vma=False)
```

```python
import jax
import jax.numpy as jnp
from jax import lax
from jax.experimental import pallas as pl
from jax.experimental.pallas import tpu as pltpu
from jax.sharding import PartitionSpec as P

MESH = pl.DeviceIdType.MESH
F32 = jnp.float32
BF16 = jnp.bfloat16

NQ, NZ, NY, NX = 4, 2, 8, 4
D = 3200
FF = 800
FP = 896
SLOT = 200
SH = 50
SHP = 64
RUN = 200
RUNP = 208
FEAT = 400
ROWS = 512
TILES = 64
QUARTER = RUNP // 4
LAST = 6 * RUNP
PACKED = LAST + 64
HALF = PACKED // 2


def by_part(m, t):
    return m == 1 and t > 2


def x_cuts(m, t):
    return ((0, HALF), (HALF, HALF)) if by_part(m, t) else ((0, 432), (432, 432), (864, 448))


def md(a, n):
    return lax.rem(a, jnp.int32(n))


def dv(a, n):
    return lax.div(a, jnp.int32(n))


def dot(a, b, dims=((1,), (0,))):
    return lax.dot_general(a, b, (dims, ((), ())), preferred_element_type=F32)


def iota(shape, dim):
    return lax.broadcasted_iota(jnp.int32, shape, dim)


def window(start):
    block = dv(start, 128) - dv(start, 3000)
    return pl.multiple_of(block * 128, 128), start - block * 128


def kernel(
    patches_hbm,
    counts,
    owners,
    plan,
    gain,
    w1,
    bias1,
    w2t,
    bias2,
    scale2,
    out,
    patches,
    rows,
    own,
    stage,
    wall,
    flat,
    normed,
    acts,
    acc,
    loc_bias,
    hidden,
    part,
    pair,
    far,
    side,
    sums_in,
    base,
    scales,
    picks,
    going,
    coming,
    turned,
    l_sem,
    st_send,
    st_recv,
    y_send,
    y_recv,
    x_send,
    x_recv,
    c_send,
    c_recv,
    s_send,
    s_recv,
    a_send,
    a_recv,
    b_send,
    b_recv,
):
    s = lax.axis_index("section")
    d = lax.axis_index("dp")
    q, c = dv(s, 2), md(s, 2)
    z, y, x = dv(d, 32), md(dv(d, 4), 8), md(d, 4)
    h = md(x + z, 2)
    e = md(x, 2)

    def dp_id(z_, y_, x_):
        return (s, z_ * 32 + y_ * 4 + x_)

    def peer(step):
        g = md(z * 4 + x + step, 8)
        return g, dv(g, 4), md(g, 4)

    def copy(src, dst, send, recv, device):
        return pltpu.make_async_remote_copy(
            src_ref=src,
            dst_ref=dst,
            send_sem=send,
            recv_sem=recv,
            device_id=device,
            device_id_type=MESH,
        )

    mate = (q * 2 + 1 - c, d)
    q_up = (md(q + 1, NQ) * 2 + c, d)
    q_dn = (md(q + NQ - 1, NQ) * 2 + c, d)
    q_far = (md(q + 2, NQ) * 2 + c, d)

    load = pltpu.make_async_copy(patches_hbm, patches, l_sem)
    load.start()

    barrier = pltpu.get_barrier_semaphore()
    for step in range(1, 8):
        _, zp, xp = peer(step)
        pl.semaphore_signal(barrier, inc=1, device_id=dp_id(zp, y, xp), device_id_type=MESH)
    for device in (dp_id(z, md(y + 1, 8), x), dp_id(z, md(y + 7, 8), x), mate, q_up, q_dn, q_far):
        pl.semaphore_signal(barrier, inc=1, device_id=device, device_id_type=MESH)

    own[...] = jnp.zeros_like(own)
    own[0, 0:SH, 0:FF] = w1[...]
    own[1, 0:SH, 0:FF] = w2t[...]

    pl.semaphore_wait(barrier, 13)

    quarters = dv(iota((RUNP, 128), 0), QUARTER) == dv(iota((RUNP, 128), 1), 32)

    def stage_copy(m, k, l):
        return copy(
            own.at[m],
            stage.at[m, x],
            st_send.at[m, 2 * k + l],
            st_recv.at[m, x],
            dp_id(md(z + l, 2), y, md(x + md(e + l, 2) + 2 * k, 4)),
        )

    def stage_start(m):
        for k in range(2):
            for l in range(2):
                if k or l:
                    stage_copy(m, k, l).start()
        pl.when(e == 1)(lambda: stage_copy(m, 0, 0).start())

        @pl.when(e == 0)
        def _():
            stage[m, x] = own[m]

    def stage_arrive(m, j):
        xs = md(x + j, 4)
        copy(own.at[m], stage.at[m, xs], st_send.at[m, 0], st_recv.at[m, xs], dp_id(z, y, x)).wait_recv()

    def stage_finish(m):
        pl.when(e == 1)(lambda: stage_arrive(m, 0))
        for j in range(1, 4):
            stage_arrive(m, j)
        row, col = iota((RUNP, 4 * SHP), 0), iota((RUNP, 4 * SHP), 1)
        pick = ((col == dv(row, SH) * SHP + md(row, SH)) & (row < RUN)).astype(BF16)
        whole = dot(pick, stage[m].reshape(4 * SHP, FP)).astype(BF16)
        for i in range(6):
            wall[m, y, h, i * RUNP : (i + 1) * RUNP, :] = whole[:, i * 128 : (i + 1) * 128]
        spread = (iota((128, 128), 0) == md(iota((128, 128), 1), 32)).astype(BF16)
        last = jnp.where(quarters, dot(whole[:, 768:FP], spread), 0.0).astype(BF16)
        fold = (iota((64, RUNP), 0) == md(iota((64, RUNP), 1), QUARTER)).astype(BF16)
        wall[m, y, h, LAST:PACKED, :] = dot(fold, last).astype(BF16)

    def unpack(m, b):
        for half in range(2):
            at = slice(half * RUNP, (half + 1) * RUNP)
            for i in range(6):
                flat[at, i * 128 : (i + 1) * 128] = wall[m, b, half, i * RUNP : (i + 1) * RUNP, :]
            unfold = (iota((RUNP, 64), 1) == md(iota((RUNP, 64), 0), QUARTER)).astype(BF16)
            last = jnp.where(quarters, dot(unfold, wall[m, b, half, LAST:PACKED, :]), 0.0).astype(BF16)
            gather = (md(iota((128, 128), 0), 32) == iota((128, 128), 1)).astype(BF16)
            flat[at, 768:FP] = dot(last, gather).astype(BF16)

    def y_copy(m, way, t, part, arriving=False):
        back = t + 1 if arriving else t
        b = md(y + 8 - back, 8) if way == 0 else md(y + back, 8)
        to = md(y + 1, 8) if way == 0 else md(y + 7, 8)
        ref = wall.at[m, b, h, pl.ds(part * HALF, HALF)]
        return copy(ref, ref, y_send.at[m, way, t, part], y_recv.at[m, way, t, part], dp_id(z, to, x))

    def x_copy(m, cut, b, t, arriving=False):
        to = (dp_id(z, y, md(x + 1, 4)), dp_id(z, y, md(x + 3, 4)), dp_id(1 - z, y, x))[cut]
        half = 1 - h if arriving else h
        start, size = x_cuts(m, t)[cut]
        ref = wall.at[m, b, half, pl.ds(start, size)]
        return copy(ref, ref, x_send.at[m, cut, b], x_recv.at[m, cut, b], to)

    def block_at(way, t):
        return md(y + 8 - t, 8) if way == 0 else md(y + t, 8)

    def y_parts(t):
        return [(way, part) for part in range(2) for way in range(2) if t < 3 or part == way]

    def send_y(m, t):
        if t == 0:
            for way, part in y_parts(0):
                y_copy(m, way, 0, part).start()
            return
        for way, part in y_parts(t - 1):
            y_copy(m, way, t - 1, part, True).wait_recv()
            if t < 4 and (way, part) in y_parts(t):
                y_copy(m, way, t, part).start()
            if by_part(m, t):
                x_copy(m, part, block_at(way, t), t).start()

    def send_x(m, t):
        for way in range(1 if t in (0, 4) else 2):
            for cut in range(len(x_cuts(m, t))):
                x_copy(m, cut, block_at(way, t), t).start()

    def send_block(m, t):
        send_y(m, t)
        if not by_part(m, t):
            send_x(m, t)

    def each(t, use):
        def one(way, carry):
            use(md(y + way * t + (1 - way) * (8 - t), 8), t)
            return carry

        lax.fori_loop(0, 1 if t in (0, 4) else 2, one, 0)

    def x_arrive(m, b, t):
        for cut in range(len(x_cuts(m, t))):
            x_copy(m, cut, b, t, True).wait_recv()

    def act(b, t):
        total = None
        for half in range(2):
            at, off = window(half * 1600 + b * RUN)
            row, col = iota((384, 2 * RUNP), 0), iota((384, 2 * RUNP), 1) - half * RUNP
            pick = ((row == col + off) & (col >= 0) & (col < RUN)).astype(BF16)
            term = dot(normed[:, pl.ds(at, 384)], pick)
            total = term if total is None else total + term
        acts[b] = total.astype(BF16)

    def fc1(b, t):
        x_arrive(0, b, t)
        unpack(0, b)
        acc[...] += dot(acts[b], flat[...])

    def roles(b):
        rel = md(q + NQ - dv(b, 4), NQ)
        return c == md(dv(b, 2), 2), rel, dv(b, 4) * 2 + md(b, 2), md(b, 2)

    def pair_copy(b, slot):
        return copy(part.at[b], pair.at[slot], c_send.at[slot], c_recv.at[slot], mate)

    def side_copy(j, way):
        to = q_up if way else q_dn
        return copy(side.at[j, way], sums_in.at[j, way], s_send.at[j, way], s_recv.at[j, way], to)

    def far_copy(j):
        return copy(far.at[j], sums_in.at[j, 2], s_send.at[j, 2], s_recv.at[j, 2], q_far)

    def fc2(b, t):
        x_arrive(1, b, t)
        unpack(1, b)
        term = dot(flat[...], hidden[...], ((1,), (1,))).astype(BF16)
        part[b] = term.reshape(2, RUNP, ROWS)
        mine, _, slot, _ = roles(b)

        @pl.when(jnp.logical_not(mine))
        def _():
            pair_copy(b, slot).start()

    def both(b, slot, run):
        return part[b, run].astype(F32) + pair[slot, run].astype(F32)

    def sum_send(b, t):
        mine, rel, slot, j = roles(b)

        @pl.when(mine)
        def _():
            pair_copy(b, slot).wait_recv()

            @pl.when(md(rel, 2) == 0)
            def _():
                far[j] = both(b, slot, 1 - dv(rel, 2)).astype(BF16)
                far_copy(j).start()

            @pl.when(md(rel, 2) == 1)
            def _():
                side[j, 0] = both(b, slot, dv(rel, 2)).astype(BF16)
                side_copy(j, 0).start()
                side[j, 1] = both(b, slot, 1 - dv(rel, 2)).astype(BF16)
                side_copy(j, 1).start()

    def sum_end(b, t):
        mine, rel, slot, j = roles(b)

        @pl.when(mine & (md(rel, 2) == 0))
        def _():
            total = both(b, slot, dv(rel, 2))
            for way in range(3):
                (far_copy(j) if way == 2 else side_copy(j, way)).wait_recv()
                total = total + sums_in[j, way].astype(F32)
            encoded = (base[j] + scales[j] * total).astype(BF16)
            for step in (4, 3, 5, 2, 6, 1, 7, 0):
                to = md(y + step, 8)
                placed = dot(encoded, picks[to], ((1,), (1,))).astype(BF16)
                if step:
                    going[j, to] = placed
                    a_copy(j, step).start()
                else:
                    coming[j, y] = placed

    def a_copy(j, step, arriving=False):
        to = md(y + step, 8)
        src = md(y + 8 - step, 8) if arriving else y
        return copy(
            going.at[j, to], coming.at[j, src], a_send.at[j, step], a_recv.at[j, step], dp_id(z, to, x)
        )

    stage_start(0)

    for i, ref in enumerate((gain, bias2, scale2)):
        rows[i : i + 1, :] = ref[...].reshape(1, D)

    stage_finish(0)
    send_block(0, 0)
    stage_start(1)

    load.wait()

    def norm(i, carry):
        at = pl.ds(pl.multiple_of(i * 64, 64), 64)
        values = patches[at, :].astype(F32)
        scale = lax.rsqrt(jnp.mean(values * values, axis=1, keepdims=True) + 1e-06)
        normed[at, :] = (values * scale * rows[0:1, :]).astype(BF16)
        return carry

    lax.fori_loop(0, 8, norm, 0)
    acc[...] = jnp.zeros_like(acc)
    each(0, act)

    send_block(0, 1)
    each(0, fc1)
    stage_finish(1)
    each(1, act)

    loc_bias[...] = jnp.zeros_like(loc_bias)
    for k in range(4):
        held = jnp.zeros((1, SLOT), F32)
        for p in range(32):
            held = jnp.where(plan[k, s] == p, bias1[p * SLOT : (p + 1) * SLOT].reshape(1, SLOT), held)
        loc_bias[:, k * SLOT : (k + 1) * SLOT] = held

    send_block(0, 2)
    each(1, fc1)
    each(2, act)
    each(3, act)
    each(4, act)

    owner_row = owners[...]
    eye = iota((TILES, TILES), 0) == iota((TILES, TILES), 1)
    owner = jnp.sum(jnp.where(eye, owner_row, 0).astype(F32), axis=1, keepdims=True).astype(jnp.int32)
    earlier = iota((TILES, TILES), 0) > iota((TILES, TILES), 1)
    rank = jnp.sum(((owner == owner_row) & earlier).astype(F32), axis=1, keepdims=True).astype(jnp.int32)
    tile = iota((TILES, 1), 0)
    count = jnp.zeros((TILES, 1), jnp.int32)
    for i in range(8):
        count = jnp.where(dv(tile, 8) == i, counts[i], count)
    place = md(dv(owner, 4), 8) * 128 + (dv(owner, 32) * 4 + md(owner, 4)) * 16 + rank * 8
    place = jnp.where(md(tile, 8) < count, place, -4096)
    token = iota((TILES, ROWS), 1)
    spread = jnp.where(iota((TILES, ROWS), 0) == dv(token, 8), place, 0).astype(F32)
    target = jnp.sum(spread, axis=0, keepdims=True).astype(jnp.int32) + md(iota((1, ROWS), 1), 8)
    for to in range(8):
        picks[to] = (target == iota((128, ROWS), 0) + to * 128).astype(BF16)

    send_block(0, 3)
    send_y(1, 0)
    each(2, fc1)

    for j in range(2):
        at, off = window(s * FEAT + j * RUN)
        row, col = iota((RUNP, 384), 0), iota((RUNP, 384), 1)
        chosen = (col == row + off) & (row < RUN)
        values = dot(chosen.astype(BF16), patches[:, pl.ds(at, 384)], ((1,), (1,)))
        bias, scale = (
            jnp.sum(jnp.where(chosen, rows[i : i + 1, pl.ds(at, 384)], 0.0), axis=1, keepdims=True)
            for i in (1, 2)
        )
        base[j] = values + scale * bias
        scales[j] = scale

    send_block(0, 4)
    send_x(1, 0)
    each(3, fc1)
    each(4, fc1)

    def gelu(i, carry):
        at = pl.ds(pl.multiple_of(i * 64, 64), 64)
        pre = acc[at, :] + loc_bias[...]
        hidden[at, :] = (0.5 * pre * (1.0 + lax.erf(pre * 0.7071067811865476))).astype(BF16)
        return carry

    lax.fori_loop(0, 4, gelu, 0)
    send_block(1, 1)
    lax.fori_loop(4, 8, gelu, 0)

    each(0, fc2)
    each(0, sum_send)
    each(1, fc2)
    send_block(1, 2)
    each(1, sum_send)
    send_block(1, 3)
    each(2, fc2)
    each(2, sum_send)
    send_block(1, 4)
    each(3, fc2)
    each(3, sum_send)
    each(4, fc2)
    each(4, sum_send)

    for m in range(2):
        for k in range(2):
            for l in range(2):
                if k or l:
                    stage_copy(m, k, l).wait_send()
        pl.when(e == 1)(lambda: stage_copy(m, 0, 0).wait_send())
        for t in range(4):
            for way, piece in y_parts(t):
                y_copy(m, way, t, piece).wait_send()
        for t in range(5):
            for way in range(1 if t in (0, 4) else 2):
                for cut in range(len(x_cuts(m, t))):
                    x_copy(m, cut, block_at(way, t), t).wait_send()

    for t in range(5):
        each(t, sum_end)

    def b_copy(step, src):
        g, zp, xp = peer(step)
        return copy(turned.at[g, src], out.at[z, src, x], b_send.at[step], b_recv.at[step], dp_id(zp, y, xp))

    def b_all(step):
        g, zp, xp = peer(8 - step)
        return copy(turned.at[g], out.at[zp, :, xp], b_send.at[step], b_recv.at[step], dp_id(zp, y, xp))

    def turn(i, carry):
        odd = md(i, 2)
        src = md(2 * md(s, 4) + odd * dv(i + 1, 2) + (1 - odd) * (8 - dv(i, 2)), 8)
        step = md(y + 8 - src, 8)

        @pl.when(step > 0)
        def _():
            for j in range(2):
                a_copy(j, step, True).wait_recv()

        block = None
        for j in range(2):
            keep = (iota((RUNP, FEAT), 1) == iota((RUNP, FEAT), 0) + j * RUN) & (iota((RUNP, FEAT), 0) < RUN)
            term = dot(coming[j, src], keep.astype(BF16), ((0,), (0,)))
            block = term if block is None else block + term
        turned[:, src] = block.astype(BF16).reshape(8, 16, FEAT)

        def send(step, carry):
            b_copy(step, src).start()
            return carry

        return lax.fori_loop(1, 8, send, carry)

    lax.fori_loop(0, 8, turn, 0)

    out[z, :, x] = turned[z * 4 + x]

    for step in range(1, 8):
        b_all(step).wait_recv()
    for step in range(1, 8):
        b_all(step).wait_send()
    for slot in range(4):
        pair_copy(0, slot).wait_send()
    for j in range(2):
        for way in range(2):
            side_copy(j, way).wait_send()
        far_copy(j).wait_send()
        for step in range(1, 8):
            a_copy(j, step).wait_send()


def local(
    patches,
    tile_counts,
    owners,
    plan,
    norm_gain,
    fc1_weight,
    fc1_bias,
    fc2_weight,
    fc2_bias,
    layer_scale,
):
    width = patches.shape[2]
    vmem = pl.BlockSpec(memory_space=pltpu.VMEM)
    smem = pl.BlockSpec(memory_space=pltpu.SMEM)
    dma = pltpu.SemaphoreType.DMA
    received = pl.pallas_call(
        kernel,
        out_shape=jax.ShapeDtypeStruct((NZ, NY, NX, 16, FEAT), BF16),
        in_specs=[pl.BlockSpec(memory_space=pl.ANY), smem, vmem, smem] + [vmem] * 6,
        out_specs=vmem,
        scratch_shapes=[
            pltpu.VMEM((ROWS, D), BF16),
            pltpu.VMEM((8, D), F32),
            pltpu.VMEM((2, SHP, FP), BF16),
            pltpu.VMEM((2, 4, SHP, FP), BF16),
            pltpu.VMEM((2, 8, 2, PACKED, 128), BF16),
            pltpu.VMEM((2 * RUNP, FP), BF16),
            pltpu.VMEM((ROWS, D), BF16),
            pltpu.VMEM((8, ROWS, 2 * RUNP), BF16),
            pltpu.VMEM((ROWS, FP), F32),
            pltpu.VMEM((1, FP), F32),
            pltpu.VMEM((ROWS, FP), BF16),
            pltpu.VMEM((8, 2, RUNP, ROWS), BF16),
            pltpu.VMEM((4, 2, RUNP, ROWS), BF16),
            pltpu.VMEM((2, RUNP, ROWS), BF16),
            pltpu.VMEM((2, 2, RUNP, ROWS), BF16),
            pltpu.VMEM((2, 3, RUNP, ROWS), BF16),
            pltpu.VMEM((2, RUNP, ROWS), F32),
            pltpu.VMEM((2, RUNP, 1), F32),
            pltpu.VMEM((8, 128, ROWS), BF16),
            pltpu.VMEM((2, 8, RUNP, 128), BF16),
            pltpu.VMEM((2, 8, RUNP, 128), BF16),
            pltpu.VMEM((8, 8, 16, FEAT), BF16),
            dma,
            dma((2, 4)),
            dma((2, 4)),
            dma((2, 2, 4, 2)),
            dma((2, 2, 4, 2)),
            dma((2, 3, 8)),
            dma((2, 3, 8)),
            dma((4,)),
            dma((4,)),
            dma((2, 3)),
            dma((2, 3)),
            dma((2, 8)),
            dma((2, 8)),
            dma((8,)),
            dma((8,)),
        ],
        compiler_params=pltpu.CompilerParams(
            collective_id=0, has_side_effects=True, vmem_limit_bytes=56 * 1024 * 1024
        ),
    )(
        patches.reshape(ROWS, width),
        tile_counts,
        owners.T,
        plan.T,
        norm_gain,
        fc1_weight,
        fc1_bias,
        fc2_weight.T,
        fc2_bias,
        layer_scale,
    )
    return received.reshape(NZ * NY * NX * 16, FEAT)


def solution(mesh):
    in_specs = (
        P("dp", None, None),
        P("dp"),
        P("dp", None),
        P(),
        P(),
        P("dp", "section"),
        P(),
        P("section", "dp"),
        P(),
        P(),
    )
    out_specs = P("dp", "section")
    return jax.shard_map(local, mesh=mesh, in_specs=in_specs, out_specs=out_specs, check_vma=False)
```

```python
import jax
import jax.numpy as jnp
from jax import lax
from jax.experimental import pallas as pl
from jax.experimental.pallas import tpu as pltpu
from jax.sharding import PartitionSpec as P

MESH = pl.DeviceIdType.MESH
F32 = jnp.float32
BF16 = jnp.bfloat16

NQ, NZ, NY, NX = 4, 2, 8, 4
D = 3200
FF = 800
FP = 896
SLOT = 200
SH = 50
SHP = 64
RUN = 200
RUNP = 208
FEAT = 400
ROWS = 512
TOK = 256
RELAYED = 1
TILES = 64
QUARTER = RUNP // 4
LAST = 6 * RUNP
PACKED = LAST + 64
HALF = PACKED // 2


def by_part(m, t):
    return m == 1 and t > 1


def x_cuts(m, t):
    return ((0, HALF), (HALF, HALF)) if by_part(m, t) else ((0, 432), (432, 432), (864, 448))


def md(a, n):
    return lax.rem(a, jnp.int32(n))


def dv(a, n):
    return lax.div(a, jnp.int32(n))


def dot(a, b, dims=((1,), (0,))):
    return lax.dot_general(a, b, (dims, ((), ())), preferred_element_type=F32)


def iota(shape, dim):
    return lax.broadcasted_iota(jnp.int32, shape, dim)


def window(start):
    block = dv(start, 128) - dv(start, 3000)
    return pl.multiple_of(block * 128, 128), start - block * 128


def kernel(
    patches_hbm,
    counts,
    owners,
    plan,
    gain,
    w1,
    bias1,
    w2t,
    bias2,
    scale2,
    out,
    patches,
    rows,
    own,
    stage,
    wall,
    flat,
    normed,
    acts,
    acc,
    loc_bias,
    hidden,
    part,
    pair,
    far,
    far_in,
    side,
    sums_in,
    base,
    scales,
    picks,
    going,
    coming,
    turned,
    quarters,
    unfold,
    gather,
    keeps,
    l_sem,
    st_send,
    st_recv,
    y_send,
    y_recv,
    x_send,
    x_recv,
    c_send,
    c_recv,
    f_send,
    f_recv,
    s_send,
    s_recv,
    a_send,
    a_recv,
    b_send,
    b_recv,
):
    s = lax.axis_index("section")
    d = lax.axis_index("dp")
    q, c = dv(s, 2), md(s, 2)
    z, y, x = dv(d, 32), md(dv(d, 4), 8), md(d, 4)
    h = md(x + z, 2)
    e = md(x, 2)

    def dp_id(z_, y_, x_):
        return (s, z_ * 32 + y_ * 4 + x_)

    def peer(step):
        g = md(z * 4 + x + step, 8)
        return g, dv(g, 4), md(g, 4)

    def copy(src, dst, send, recv, device):
        return pltpu.make_async_remote_copy(
            src_ref=src,
            dst_ref=dst,
            send_sem=send,
            recv_sem=recv,
            device_id=device,
            device_id_type=MESH,
        )

    mate = (q * 2 + 1 - c, d)
    q_up = (md(q + 1, NQ) * 2 + c, d)
    q_dn = (md(q + NQ - 1, NQ) * 2 + c, d)
    q_far = (md(q + 2, NQ) * 2 + c, d)

    load = pltpu.make_async_copy(patches_hbm, patches, l_sem)
    load.start()

    barrier = pltpu.get_barrier_semaphore()
    for step in range(1, 8):
        _, zp, xp = peer(step)
        pl.semaphore_signal(barrier, inc=1, device_id=dp_id(zp, y, xp), device_id_type=MESH)
    for device in (dp_id(z, md(y + 1, 8), x), dp_id(z, md(y + 7, 8), x), mate, q_up, q_dn, q_far):
        pl.semaphore_signal(barrier, inc=1, device_id=device, device_id_type=MESH)

    own[...] = jnp.zeros_like(own)
    own[0, 0:SH, 0:FF] = w1[...]
    own[1, 0:SH, 0:FF] = w2t[...]

    quarters[...] = (dv(iota((RUNP, 128), 0), QUARTER) == dv(iota((RUNP, 128), 1), 32)).astype(F32)
    unfold[...] = (iota((RUNP, 64), 1) == md(iota((RUNP, 64), 0), QUARTER)).astype(BF16)
    gather[...] = (md(iota((128, 128), 0), 32) == iota((128, 128), 1)).astype(BF16)
    for j in range(2):
        row, col = iota((RUNP, FEAT), 0), iota((RUNP, FEAT), 1)
        keeps[j] = ((col == row + j * RUN) & (row < RUN)).astype(BF16)

    pl.semaphore_wait(barrier, 13)


    def stage_copy(m, k, l):
        return copy(
            own.at[m],
            stage.at[m, x],
            st_send.at[m, 2 * k + l],
            st_recv.at[m, x],
            dp_id(md(z + l, 2), y, md(x + md(e + l, 2) + 2 * k, 4)),
        )

    def stage_start(m):
        for k in range(2):
            for l in range(2):
                if k or l:
                    stage_copy(m, k, l).start()
        pl.when(e == 1)(lambda: stage_copy(m, 0, 0).start())

        @pl.when(e == 0)
        def _():
            stage[m, x] = own[m]

    def stage_arrive(m, j):
        xs = md(x + j, 4)
        copy(own.at[m], stage.at[m, xs], st_send.at[m, 0], st_recv.at[m, xs], dp_id(z, y, x)).wait_recv()

    def stage_finish(m):
        pl.when(e == 1)(lambda: stage_arrive(m, 0))
        for j in range(1, 4):
            stage_arrive(m, j)
        row, col = iota((RUNP, 4 * SHP), 0), iota((RUNP, 4 * SHP), 1)
        pick = ((col == dv(row, SH) * SHP + md(row, SH)) & (row < RUN)).astype(BF16)
        whole = dot(pick, stage[m].reshape(4 * SHP, FP)).astype(BF16)
        for i in range(6):
            wall[m, y, h, i * RUNP : (i + 1) * RUNP, :] = whole[:, i * 128 : (i + 1) * 128]
        spread = (iota((128, 128), 0) == md(iota((128, 128), 1), 32)).astype(BF16)
        last = (dot(whole[:, 768:FP], spread) * quarters[...]).astype(BF16)
        fold = (iota((64, RUNP), 0) == md(iota((64, RUNP), 1), QUARTER)).astype(BF16)
        wall[m, y, h, LAST:PACKED, :] = dot(fold, last).astype(BF16)

    def unpack(m, b):
        for half in range(2):
            at = slice(half * RUNP, (half + 1) * RUNP)
            for i in range(6):
                flat[at, i * 128 : (i + 1) * 128] = wall[m, b, half, i * RUNP : (i + 1) * RUNP, :]
            last = (dot(unfold[...], wall[m, b, half, LAST:PACKED, :]) * quarters[...]).astype(BF16)
            flat[at, 768:FP] = dot(last, gather[...]).astype(BF16)

    def y_copy(m, way, t, part, arriving=False):
        back = t + 1 if arriving else t
        b = md(y + 8 - back, 8) if way == 0 else md(y + back, 8)
        to = md(y + 1, 8) if way == 0 else md(y + 7, 8)
        ref = wall.at[m, b, h, pl.ds(part * HALF, HALF)]
        return copy(ref, ref, y_send.at[m, way, t, part], y_recv.at[m, way, t, part], dp_id(z, to, x))

    def x_copy(m, cut, b, t, arriving=False):
        to = (dp_id(z, y, md(x + 1, 4)), dp_id(z, y, md(x + 3, 4)), dp_id(1 - z, y, x))[cut]
        half = 1 - h if arriving else h
        start, size = x_cuts(m, t)[cut]
        ref = wall.at[m, b, half, pl.ds(start, size)]
        return copy(ref, ref, x_send.at[m, cut, b], x_recv.at[m, cut, b], to)

    def block_at(way, t):
        return md(y + 8 - t, 8) if way == 0 else md(y + t, 8)

    def y_parts(t):
        return [(way, part) for part in range(2) for way in range(2) if t < 3 or part == way]

    def send_y(m, t):
        if t == 0:
            for way, part in y_parts(0):
                y_copy(m, way, 0, part).start()
            return
        for way, part in y_parts(t - 1):
            y_copy(m, way, t - 1, part, True).wait_recv()
            if t < 4 and (way, part) in y_parts(t):
                y_copy(m, way, t, part).start()
            if by_part(m, t):
                x_copy(m, part, block_at(way, t), t).start()

    def send_x(m, t):
        for way in range(1 if t in (0, 4) else 2):
            for cut in range(len(x_cuts(m, t))):
                x_copy(m, cut, block_at(way, t), t).start()

    def send_block(m, t):
        send_y(m, t)
        if not by_part(m, t):
            send_x(m, t)

    def each(t, use):
        def one(way, carry):
            use(md(y + way * t + (1 - way) * (8 - t), 8), t)
            return carry

        lax.fori_loop(0, 1 if t in (0, 4) else 2, one, 0)

    def x_arrive(m, b, t):
        for cut in range(len(x_cuts(m, t))):
            x_copy(m, cut, b, t, True).wait_recv()

    def act(b, t):
        total = None
        for half in range(2):
            at, off = window(half * 1600 + b * RUN)
            row, col = iota((384, 2 * RUNP), 0), iota((384, 2 * RUNP), 1) - half * RUNP
            pick = ((row == col + off) & (col >= 0) & (col < RUN)).astype(BF16)
            term = dot(normed[:, pl.ds(at, 384)], pick)
            total = term if total is None else total + term
        acts[b] = total.astype(BF16)

    def fc1(b, t):
        x_arrive(0, b, t)
        unpack(0, b)
        acc[...] += dot(acts[b], flat[...])

    def roles(b):
        rel = md(q + NQ - dv(b, 4), NQ)
        return c == md(dv(b, 2), 2), rel, dv(b, 4) * 2 + md(b, 2), md(b, 2)

    def pair_copy(b, slot):
        return copy(part.at[b], pair.at[slot], c_send.at[slot], c_recv.at[slot], mate)

    def side_copy(j, way):
        to = q_up if way else q_dn
        return copy(side.at[j, way], sums_in.at[j, way], s_send.at[j, way], s_recv.at[j, way], to)

    def near_copy(j, half):
        return copy(
            far.at[j, :, pl.ds(half * TOK, TOK)],
            far_in.at[j, half],
            f_send.at[j, half],
            f_recv.at[j, half],
            q_up if half else q_dn,
        )

    def far_copy(j):
        return copy(far.at[j], sums_in.at[j, 2], s_send.at[j, 2], s_recv.at[j, 2], q_far)

    def fc2(b, t):
        x_arrive(1, b, t)
        unpack(1, b)
        term = dot(flat[...], hidden[...], ((1,), (1,))).astype(BF16)
        part[b] = term.reshape(2, RUNP, ROWS)
        mine, _, slot, _ = roles(b)

        @pl.when(jnp.logical_not(mine))
        def _():
            pair_copy(b, slot).start()

    def both(b, slot, run):
        return part[b, run].astype(F32) + pair[slot, run].astype(F32)

    def sum_send(b, t):
        mine, rel, slot, j = roles(b)

        @pl.when(mine)
        def _():
            pair_copy(b, slot).wait_recv()

            @pl.when(md(rel, 2) == 0)
            def _():
                far[j] = both(b, slot, 1 - dv(rel, 2)).astype(BF16)
                if t > RELAYED:
                    far_copy(j).start()
                else:
                    near_copy(j, 0).start()
                    near_copy(j, 1).start()

            if t > RELAYED:

                @pl.when(md(rel, 2) == 1)
                def _():
                    side[j, 0] = both(b, slot, dv(rel, 2)).astype(BF16)
                    side_copy(j, 0).start()
                    side[j, 1] = both(b, slot, 1 - dv(rel, 2)).astype(BF16)
                    side_copy(j, 1).start()

    def sum_relay(b, t):
        mine, rel, slot, j = roles(b)

        @pl.when(mine & (md(rel, 2) == 1))
        def _():
            for way in range(2):
                near_copy(j, way).wait_recv()
                total = both(b, slot, dv(rel, 2) if way == 0 else 1 - dv(rel, 2))
                lo, hi = total[:, 0:TOK], total[:, TOK:ROWS]
                if way == 0:
                    lo = lo + far_in[j, 0].astype(F32)
                else:
                    hi = hi + far_in[j, 1].astype(F32)
                side[j, way, :, 0:TOK] = lo.astype(BF16)
                side[j, way, :, TOK:ROWS] = hi.astype(BF16)
                side_copy(j, way).start()

    def sum_end(b, t):
        mine, rel, slot, j = roles(b)

        @pl.when(mine & (md(rel, 2) == 0))
        def _():
            total = both(b, slot, dv(rel, 2))
            for way in range(3 if t > RELAYED else 2):
                (far_copy(j) if way == 2 else side_copy(j, way)).wait_recv()
                total = total + sums_in[j, way].astype(F32)
            encoded = (base[j] + scales[j] * total).astype(BF16)
            for step in (4, 3, 5, 2, 6, 1, 7, 0):
                to = md(y + step, 8)
                placed = dot(encoded, picks[to], ((1,), (1,))).astype(BF16)
                if step:
                    going[j, to] = placed
                    a_copy(j, step).start()
                else:
                    coming[j, y] = placed
            if t > RELAYED:
                far_copy(j).wait_send()
            else:
                near_copy(j, 0).wait_send()
                near_copy(j, 1).wait_send()

    def a_copy(j, step, arriving=False):
        to = md(y + step, 8)
        src = md(y + 8 - step, 8) if arriving else y
        return copy(
            going.at[j, to], coming.at[j, src], a_send.at[j, step], a_recv.at[j, step], dp_id(z, to, x)
        )

    stage_start(0)

    for i, ref in enumerate((gain, bias2, scale2)):
        rows[i : i + 1, :] = ref[...].reshape(1, D)

    stage_finish(0)
    send_block(0, 0)
    stage_start(1)

    load.wait()

    def norm(i, carry):
        at = pl.ds(pl.multiple_of(i * 64, 64), 64)
        values = patches[at, :].astype(F32)
        scale = lax.rsqrt(jnp.mean(values * values, axis=1, keepdims=True) + 1e-06)
        normed[at, :] = (values * scale * rows[0:1, :]).astype(BF16)
        return carry

    lax.fori_loop(0, 8, norm, 0)
    acc[...] = jnp.zeros_like(acc)
    each(0, act)

    send_block(0, 1)
    each(0, fc1)
    stage_finish(1)
    each(1, act)

    loc_bias[...] = jnp.zeros_like(loc_bias)
    for k in range(4):
        held = jnp.zeros((1, SLOT), F32)
        for p in range(32):
            held = jnp.where(plan[k, s] == p, bias1[p * SLOT : (p + 1) * SLOT].reshape(1, SLOT), held)
        loc_bias[:, k * SLOT : (k + 1) * SLOT] = held

    send_block(0, 2)
    each(1, fc1)
    each(2, act)
    each(3, act)
    each(4, act)

    owner_row = owners[...]
    eye = iota((TILES, TILES), 0) == iota((TILES, TILES), 1)
    owner = jnp.sum(jnp.where(eye, owner_row, 0).astype(F32), axis=1, keepdims=True).astype(jnp.int32)
    earlier = iota((TILES, TILES), 0) > iota((TILES, TILES), 1)
    rank = jnp.sum(((owner == owner_row) & earlier).astype(F32), axis=1, keepdims=True).astype(jnp.int32)
    tile = iota((TILES, 1), 0)
    count = jnp.zeros((TILES, 1), jnp.int32)
    for i in range(8):
        count = jnp.where(dv(tile, 8) == i, counts[i], count)
    place = md(dv(owner, 4), 8) * 128 + (dv(owner, 32) * 4 + md(owner, 4)) * 16 + rank * 8
    place = jnp.where(md(tile, 8) < count, place, -4096)
    token = iota((TILES, ROWS), 1)
    spread = jnp.where(iota((TILES, ROWS), 0) == dv(token, 8), place, 0).astype(F32)
    target = jnp.sum(spread, axis=0, keepdims=True).astype(jnp.int32) + md(iota((1, ROWS), 1), 8)
    for to in range(8):
        picks[to] = (target == iota((128, ROWS), 0) + to * 128).astype(BF16)

    send_block(0, 3)
    send_y(1, 0)
    each(2, fc1)

    for j in range(2):
        at, off = window(s * FEAT + j * RUN)
        row, col = iota((RUNP, 384), 0), iota((RUNP, 384), 1)
        chosen = (col == row + off) & (row < RUN)
        values = dot(chosen.astype(BF16), patches[:, pl.ds(at, 384)], ((1,), (1,)))
        bias, scale = (
            jnp.sum(jnp.where(chosen, rows[i : i + 1, pl.ds(at, 384)], 0.0), axis=1, keepdims=True)
            for i in (1, 2)
        )
        base[j] = values + scale * bias
        scales[j] = scale

    send_block(0, 4)
    send_x(1, 0)
    each(3, fc1)
    each(4, fc1)

    def gelu(i, carry):
        at = pl.ds(pl.multiple_of(i * 64, 64), 64)
        pre = acc[at, :] + loc_bias[...]
        hidden[at, :] = (0.5 * pre * (1.0 + lax.erf(pre * 0.7071067811865476))).astype(BF16)
        return carry

    lax.fori_loop(0, 4, gelu, 0)
    send_block(1, 1)
    lax.fori_loop(4, 8, gelu, 0)

    each(0, fc2)
    each(1, fc2)
    each(0, sum_send)
    send_block(1, 2)
    each(1, sum_send)
    each(0, sum_relay)
    each(1, sum_relay)
    send_block(1, 3)
    each(2, fc2)
    each(2, sum_send)
    send_block(1, 4)
    each(3, fc2)
    each(4, fc2)
    each(3, sum_send)
    each(4, sum_send)

    for m in range(2):
        for k in range(2):
            for l in range(2):
                if k or l:
                    stage_copy(m, k, l).wait_send()
        pl.when(e == 1)(lambda: stage_copy(m, 0, 0).wait_send())
        for t in range(4):
            for way, piece in y_parts(t):
                y_copy(m, way, t, piece).wait_send()
        for t in range(5):
            for way in range(1 if t in (0, 4) else 2):
                for cut in range(len(x_cuts(m, t))):
                    x_copy(m, cut, block_at(way, t), t).wait_send()

    for t in range(5):
        each(t, sum_end)

    def b_copy(step, src):
        g, zp, xp = peer(step)
        return copy(turned.at[g, src], out.at[z, src, x], b_send.at[step], b_recv.at[step], dp_id(zp, y, xp))

    def b_all(step):
        g, zp, xp = peer(8 - step)
        return copy(turned.at[g], out.at[zp, :, xp], b_send.at[step], b_recv.at[step], dp_id(zp, y, xp))

    def turn(i, carry):
        odd = md(i, 2)
        src = md(2 * md(s, 4) + odd * dv(i + 1, 2) + (1 - odd) * (8 - dv(i, 2)), 8)
        step = md(y + 8 - src, 8)

        @pl.when(step > 0)
        def _():
            for j in range(2):
                a_copy(j, step, True).wait_recv()

        block = None
        for j in range(2):
            term = dot(coming[j, src], keeps[j], ((0,), (0,)))
            block = term if block is None else block + term
        turned[:, src] = block.astype(BF16).reshape(8, 16, FEAT)

        def send(step, carry):
            b_copy(step, src).start()
            return carry

        return lax.fori_loop(1, 8, send, carry)

    lax.fori_loop(0, 8, turn, 0)

    out[z, :, x] = turned[z * 4 + x]

    for step in range(1, 8):
        b_all(step).wait_recv()
    for step in range(1, 8):
        b_all(step).wait_send()
    for slot in range(4):
        pair_copy(0, slot).wait_send()
    for j in range(2):
        for way in range(2):
            side_copy(j, way).wait_send()
        for step in range(1, 8):
            a_copy(j, step).wait_send()


def local(
    patches,
    tile_counts,
    owners,
    plan,
    norm_gain,
    fc1_weight,
    fc1_bias,
    fc2_weight,
    fc2_bias,
    layer_scale,
):
    width = patches.shape[2]
    vmem = pl.BlockSpec(memory_space=pltpu.VMEM)
    smem = pl.BlockSpec(memory_space=pltpu.SMEM)
    dma = pltpu.SemaphoreType.DMA
    received = pl.pallas_call(
        kernel,
        out_shape=jax.ShapeDtypeStruct((NZ, NY, NX, 16, FEAT), BF16),
        in_specs=[pl.BlockSpec(memory_space=pl.ANY), smem, vmem, smem] + [vmem] * 6,
        out_specs=vmem,
        scratch_shapes=[
            pltpu.VMEM((ROWS, D), BF16),
            pltpu.VMEM((8, D), F32),
            pltpu.VMEM((2, SHP, FP), BF16),
            pltpu.VMEM((2, 4, SHP, FP), BF16),
            pltpu.VMEM((2, 8, 2, PACKED, 128), BF16),
            pltpu.VMEM((2 * RUNP, FP), BF16),
            pltpu.VMEM((ROWS, D), BF16),
            pltpu.VMEM((8, ROWS, 2 * RUNP), BF16),
            pltpu.VMEM((ROWS, FP), F32),
            pltpu.VMEM((1, FP), F32),
            pltpu.VMEM((ROWS, FP), BF16),
            pltpu.VMEM((8, 2, RUNP, ROWS), BF16),
            pltpu.VMEM((4, 2, RUNP, ROWS), BF16),
            pltpu.VMEM((2, RUNP, ROWS), BF16),
            pltpu.VMEM((2, 2, RUNP, TOK), BF16),
            pltpu.VMEM((2, 2, RUNP, ROWS), BF16),
            pltpu.VMEM((2, 3, RUNP, ROWS), BF16),
            pltpu.VMEM((2, RUNP, ROWS), F32),
            pltpu.VMEM((2, RUNP, 1), F32),
            pltpu.VMEM((8, 128, ROWS), BF16),
            pltpu.VMEM((2, 8, RUNP, 128), BF16),
            pltpu.VMEM((2, 8, RUNP, 128), BF16),
            pltpu.VMEM((8, 8, 16, FEAT), BF16),
            pltpu.VMEM((RUNP, 128), F32),
            pltpu.VMEM((RUNP, 64), BF16),
            pltpu.VMEM((128, 128), BF16),
            pltpu.VMEM((2, RUNP, FEAT), BF16),
            dma,
            dma((2, 4)),
            dma((2, 4)),
            dma((2, 2, 4, 2)),
            dma((2, 2, 4, 2)),
            dma((2, 3, 8)),
            dma((2, 3, 8)),
            dma((4,)),
            dma((4,)),
            dma((2, 2)),
            dma((2, 2)),
            dma((2, 3)),
            dma((2, 3)),
            dma((2, 8)),
            dma((2, 8)),
            dma((8,)),
            dma((8,)),
        ],
        compiler_params=pltpu.CompilerParams(
            collective_id=0, has_side_effects=True, vmem_limit_bytes=56 * 1024 * 1024
        ),
    )(
        patches.reshape(ROWS, width),
        tile_counts,
        owners.T,
        plan.T,
        norm_gain,
        fc1_weight,
        fc1_bias,
        fc2_weight.T,
        fc2_bias,
        layer_scale,
    )
    return received.reshape(NZ * NY * NX * 16, FEAT)


def solution(mesh):
    in_specs = (
        P("dp", None, None),
        P("dp"),
        P("dp", None),
        P(),
        P(),
        P("dp", "section"),
        P(),
        P("section", "dp"),
        P(),
        P(),
    )
    out_specs = P("dp", "section")
    return jax.shard_map(local, mesh=mesh, in_specs=in_specs, out_specs=out_specs, check_vma=False)
```

```python
import jax
import jax.numpy as jnp
from jax import lax
from jax.experimental import pallas as pl
from jax.experimental.pallas import tpu as pltpu
from jax.sharding import PartitionSpec as P

MESH = pl.DeviceIdType.MESH
F32 = jnp.float32
BF16 = jnp.bfloat16

NQ, NZ, NY, NX = 4, 2, 8, 4
D = 3200
FF = 800
FP = 896
SLOT = 200
SH = 50
SHP = 64
RUN = 200
RUNP = 208
FEAT = 400
ROWS = 512
TOK = 256
RELAYED = 2
TILES = 64
QUARTER = RUNP // 4
LAST = 6 * RUNP
PACKED = LAST + 64
HALF = PACKED // 2


def by_part(m, t):
    return m == 1 and t > 1


def x_cuts(m, t):
    return ((0, HALF), (HALF, HALF)) if by_part(m, t) else ((0, 432), (432, 432), (864, 448))


def md(a, n):
    return lax.rem(a, jnp.int32(n))


def dv(a, n):
    return lax.div(a, jnp.int32(n))


def dot(a, b, dims=((1,), (0,))):
    return lax.dot_general(a, b, (dims, ((), ())), preferred_element_type=F32)


def iota(shape, dim):
    return lax.broadcasted_iota(jnp.int32, shape, dim)


def window(start):
    block = dv(start, 128) - dv(start, 3000)
    return pl.multiple_of(block * 128, 128), start - block * 128


def kernel(
    patches_hbm,
    counts,
    owners,
    plan,
    gain,
    w1,
    bias1,
    w2t,
    bias2,
    scale2,
    out,
    patches,
    rows,
    own,
    stage,
    wall,
    flat,
    normed,
    acts,
    acc,
    loc_bias,
    hidden,
    part,
    pair,
    far,
    far_in,
    side,
    sums_in,
    base,
    scales,
    picks,
    going,
    coming,
    turned,
    quarters,
    unfold,
    gather,
    keeps,
    l_sem,
    st_send,
    st_recv,
    y_send,
    y_recv,
    x_send,
    x_recv,
    c_send,
    c_recv,
    f_send,
    f_recv,
    s_send,
    s_recv,
    a_send,
    a_recv,
    b_send,
    b_recv,
):
    s = lax.axis_index("section")
    d = lax.axis_index("dp")
    q, c = dv(s, 2), md(s, 2)
    z, y, x = dv(d, 32), md(dv(d, 4), 8), md(d, 4)
    h = md(x + z, 2)
    e = md(x, 2)

    def dp_id(z_, y_, x_):
        return (s, z_ * 32 + y_ * 4 + x_)

    def peer(step):
        g = md(z * 4 + x + step, 8)
        return g, dv(g, 4), md(g, 4)

    def copy(src, dst, send, recv, device):
        return pltpu.make_async_remote_copy(
            src_ref=src,
            dst_ref=dst,
            send_sem=send,
            recv_sem=recv,
            device_id=device,
            device_id_type=MESH,
        )

    mate = (q * 2 + 1 - c, d)
    q_up = (md(q + 1, NQ) * 2 + c, d)
    q_dn = (md(q + NQ - 1, NQ) * 2 + c, d)
    q_far = (md(q + 2, NQ) * 2 + c, d)

    load = pltpu.make_async_copy(patches_hbm, patches, l_sem)
    load.start()

    barrier = pltpu.get_barrier_semaphore()
    for step in range(1, 8):
        _, zp, xp = peer(step)
        pl.semaphore_signal(barrier, inc=1, device_id=dp_id(zp, y, xp), device_id_type=MESH)
    for device in (dp_id(z, md(y + 1, 8), x), dp_id(z, md(y + 7, 8), x), mate, q_up, q_dn, q_far):
        pl.semaphore_signal(barrier, inc=1, device_id=device, device_id_type=MESH)

    own[...] = jnp.zeros_like(own)
    own[0, 0:SH, 0:FF] = w1[...]
    own[1, 0:SH, 0:FF] = w2t[...]

    quarters[...] = (dv(iota((RUNP, 128), 0), QUARTER) == dv(iota((RUNP, 128), 1), 32)).astype(F32)
    unfold[...] = (iota((RUNP, 64), 1) == md(iota((RUNP, 64), 0), QUARTER)).astype(BF16)
    gather[...] = (md(iota((128, 128), 0), 32) == iota((128, 128), 1)).astype(BF16)
    for j in range(2):
        row, col = iota((RUNP, FEAT), 0), iota((RUNP, FEAT), 1)
        keeps[j] = ((col == row + j * RUN) & (row < RUN)).astype(BF16)

    pl.semaphore_wait(barrier, 13)


    def stage_copy(m, k, l):
        return copy(
            own.at[m],
            stage.at[m, x],
            st_send.at[m, 2 * k + l],
            st_recv.at[m, x],
            dp_id(md(z + l, 2), y, md(x + md(e + l, 2) + 2 * k, 4)),
        )

    def stage_start(m):
        for k in range(2):
            for l in range(2):
                if k or l:
                    stage_copy(m, k, l).start()
        pl.when(e == 1)(lambda: stage_copy(m, 0, 0).start())

        @pl.when(e == 0)
        def _():
            stage[m, x] = own[m]

    def stage_arrive(m, j):
        xs = md(x + j, 4)
        copy(own.at[m], stage.at[m, xs], st_send.at[m, 0], st_recv.at[m, xs], dp_id(z, y, x)).wait_recv()

    def stage_finish(m):
        pl.when(e == 1)(lambda: stage_arrive(m, 0))
        for j in range(1, 4):
            stage_arrive(m, j)
        row, col = iota((RUNP, 4 * SHP), 0), iota((RUNP, 4 * SHP), 1)
        pick = ((col == dv(row, SH) * SHP + md(row, SH)) & (row < RUN)).astype(BF16)
        whole = dot(pick, stage[m].reshape(4 * SHP, FP)).astype(BF16)
        for i in range(6):
            wall[m, y, h, i * RUNP : (i + 1) * RUNP, :] = whole[:, i * 128 : (i + 1) * 128]
        spread = (iota((128, 128), 0) == md(iota((128, 128), 1), 32)).astype(BF16)
        last = (dot(whole[:, 768:FP], spread) * quarters[...]).astype(BF16)
        fold = (iota((64, RUNP), 0) == md(iota((64, RUNP), 1), QUARTER)).astype(BF16)
        wall[m, y, h, LAST:PACKED, :] = dot(fold, last).astype(BF16)

    def unpack(m, b):
        for half in range(2):
            at = slice(half * RUNP, (half + 1) * RUNP)
            for i in range(6):
                flat[at, i * 128 : (i + 1) * 128] = wall[m, b, half, i * RUNP : (i + 1) * RUNP, :]
            last = (dot(unfold[...], wall[m, b, half, LAST:PACKED, :]) * quarters[...]).astype(BF16)
            flat[at, 768:FP] = dot(last, gather[...]).astype(BF16)

    def y_copy(m, way, t, part, arriving=False):
        back = t + 1 if arriving else t
        b = md(y + 8 - back, 8) if way == 0 else md(y + back, 8)
        to = md(y + 1, 8) if way == 0 else md(y + 7, 8)
        ref = wall.at[m, b, h, pl.ds(part * HALF, HALF)]
        return copy(ref, ref, y_send.at[m, way, t, part], y_recv.at[m, way, t, part], dp_id(z, to, x))

    def x_copy(m, cut, b, t, arriving=False):
        to = (dp_id(z, y, md(x + 1, 4)), dp_id(z, y, md(x + 3, 4)), dp_id(1 - z, y, x))[cut]
        half = 1 - h if arriving else h
        start, size = x_cuts(m, t)[cut]
        ref = wall.at[m, b, half, pl.ds(start, size)]
        return copy(ref, ref, x_send.at[m, cut, b], x_recv.at[m, cut, b], to)

    def block_at(way, t):
        return md(y + 8 - t, 8) if way == 0 else md(y + t, 8)

    def y_parts(t):
        return [(way, part) for part in range(2) for way in range(2) if t < 3 or part == way]

    def send_y(m, t):
        if t == 0:
            for way, part in y_parts(0):
                y_copy(m, way, 0, part).start()
            return
        for way, part in y_parts(t - 1):
            y_copy(m, way, t - 1, part, True).wait_recv()
            if t < 4 and (way, part) in y_parts(t):
                y_copy(m, way, t, part).start()
            if by_part(m, t):
                x_copy(m, part, block_at(way, t), t).start()

    def send_x(m, t):
        for way in range(1 if t in (0, 4) else 2):
            for cut in range(len(x_cuts(m, t))):
                x_copy(m, cut, block_at(way, t), t).start()

    def send_block(m, t):
        send_y(m, t)
        if not by_part(m, t):
            send_x(m, t)

    def each(t, use):
        def one(way, carry):
            use(md(y + way * t + (1 - way) * (8 - t), 8), t)
            return carry

        lax.fori_loop(0, 1 if t in (0, 4) else 2, one, 0)

    def x_arrive(m, b, t):
        for cut in range(len(x_cuts(m, t))):
            x_copy(m, cut, b, t, True).wait_recv()

    def act(b, t):
        total = None
        for half in range(2):
            at, off = window(half * 1600 + b * RUN)
            row, col = iota((384, 2 * RUNP), 0), iota((384, 2 * RUNP), 1) - half * RUNP
            pick = ((row == col + off) & (col >= 0) & (col < RUN)).astype(BF16)
            term = dot(normed[:, pl.ds(at, 384)], pick)
            total = term if total is None else total + term
        acts[b] = total.astype(BF16)

    def fc1(b, t):
        x_arrive(0, b, t)
        unpack(0, b)
        acc[...] += dot(acts[b], flat[...])

    def roles(b):
        rel = md(q + NQ - dv(b, 4), NQ)
        return c == md(dv(b, 2), 2), rel, dv(b, 4) * 2 + md(b, 2), md(b, 2)

    def pair_copy(b, slot):
        return copy(part.at[b], pair.at[slot], c_send.at[slot], c_recv.at[slot], mate)

    def side_copy(j, way):
        to = q_up if way else q_dn
        return copy(side.at[j, way], sums_in.at[j, way], s_send.at[j, way], s_recv.at[j, way], to)

    def near_copy(j, half):
        return copy(
            far.at[j, :, pl.ds(half * TOK, TOK)],
            far_in.at[j, half],
            f_send.at[j, half],
            f_recv.at[j, half],
            q_up if half else q_dn,
        )

    def far_copy(j):
        return copy(far.at[j], sums_in.at[j, 2], s_send.at[j, 2], s_recv.at[j, 2], q_far)

    def fc2(b, t):
        x_arrive(1, b, t)
        unpack(1, b)
        term = dot(flat[...], hidden[...], ((1,), (1,))).astype(BF16)
        part[b] = term.reshape(2, RUNP, ROWS)
        mine, _, slot, _ = roles(b)

        @pl.when(jnp.logical_not(mine))
        def _():
            pair_copy(b, slot).start()

    def both(b, slot, run):
        return part[b, run].astype(F32) + pair[slot, run].astype(F32)

    def sum_send(b, t):
        mine, rel, slot, j = roles(b)

        @pl.when(mine)
        def _():
            pair_copy(b, slot).wait_recv()

            @pl.when(md(rel, 2) == 0)
            def _():
                far[j] = both(b, slot, 1 - dv(rel, 2)).astype(BF16)
                if t > RELAYED:
                    far_copy(j).start()
                else:
                    near_copy(j, 0).start()
                    near_copy(j, 1).start()

            if t > RELAYED:

                @pl.when(md(rel, 2) == 1)
                def _():
                    side[j, 0] = both(b, slot, dv(rel, 2)).astype(BF16)
                    side_copy(j, 0).start()
                    side[j, 1] = both(b, slot, 1 - dv(rel, 2)).astype(BF16)
                    side_copy(j, 1).start()

    def sum_relay(b, t):
        mine, rel, slot, j = roles(b)

        @pl.when(mine & (md(rel, 2) == 1))
        def _():
            for way in range(2):
                near_copy(j, way).wait_recv()
                total = both(b, slot, dv(rel, 2) if way == 0 else 1 - dv(rel, 2))
                lo, hi = total[:, 0:TOK], total[:, TOK:ROWS]
                if way == 0:
                    lo = lo + far_in[j, 0].astype(F32)
                else:
                    hi = hi + far_in[j, 1].astype(F32)
                side[j, way, :, 0:TOK] = lo.astype(BF16)
                side[j, way, :, TOK:ROWS] = hi.astype(BF16)
                side_copy(j, way).start()

    def sum_end(b, t):
        mine, rel, slot, j = roles(b)

        @pl.when(mine & (md(rel, 2) == 0))
        def _():
            total = both(b, slot, dv(rel, 2))
            for way in range(3 if t > RELAYED else 2):
                (far_copy(j) if way == 2 else side_copy(j, way)).wait_recv()
                total = total + sums_in[j, way].astype(F32)
            encoded = (base[j] + scales[j] * total).astype(BF16)
            for step in (4, 3, 5, 2, 6, 1, 7, 0):
                to = md(y + step, 8)
                placed = dot(encoded, picks[to], ((1,), (1,))).astype(BF16)
                if step:
                    going[j, to] = placed
                    a_copy(j, step).start()
                else:
                    coming[j, y] = placed
            if t > RELAYED:
                far_copy(j).wait_send()
            else:
                near_copy(j, 0).wait_send()
                near_copy(j, 1).wait_send()

    def a_copy(j, step, arriving=False):
        to = md(y + step, 8)
        src = md(y + 8 - step, 8) if arriving else y
        return copy(
            going.at[j, to], coming.at[j, src], a_send.at[j, step], a_recv.at[j, step], dp_id(z, to, x)
        )

    stage_start(0)

    for i, ref in enumerate((gain, bias2, scale2)):
        rows[i : i + 1, :] = ref[...].reshape(1, D)

    stage_finish(0)
    send_block(0, 0)
    stage_start(1)

    load.wait()

    def norm(i, carry):
        at = pl.ds(pl.multiple_of(i * 64, 64), 64)
        values = patches[at, :].astype(F32)
        scale = lax.rsqrt(jnp.mean(values * values, axis=1, keepdims=True) + 1e-06)
        normed[at, :] = (values * scale * rows[0:1, :]).astype(BF16)
        return carry

    lax.fori_loop(0, 8, norm, 0)
    acc[...] = jnp.zeros_like(acc)
    each(0, act)

    send_block(0, 1)
    each(0, fc1)
    stage_finish(1)
    each(1, act)

    loc_bias[...] = jnp.zeros_like(loc_bias)
    for k in range(4):
        held = jnp.zeros((1, SLOT), F32)
        for p in range(32):
            held = jnp.where(plan[k, s] == p, bias1[p * SLOT : (p + 1) * SLOT].reshape(1, SLOT), held)
        loc_bias[:, k * SLOT : (k + 1) * SLOT] = held

    send_block(0, 2)
    each(1, fc1)
    each(2, act)
    each(3, act)
    each(4, act)

    owner_row = owners[...]
    eye = iota((TILES, TILES), 0) == iota((TILES, TILES), 1)
    owner = jnp.sum(jnp.where(eye, owner_row, 0).astype(F32), axis=1, keepdims=True).astype(jnp.int32)
    earlier = iota((TILES, TILES), 0) > iota((TILES, TILES), 1)
    rank = jnp.sum(((owner == owner_row) & earlier).astype(F32), axis=1, keepdims=True).astype(jnp.int32)
    tile = iota((TILES, 1), 0)
    count = jnp.zeros((TILES, 1), jnp.int32)
    for i in range(8):
        count = jnp.where(dv(tile, 8) == i, counts[i], count)
    place = md(dv(owner, 4), 8) * 128 + (dv(owner, 32) * 4 + md(owner, 4)) * 16 + rank * 8
    place = jnp.where(md(tile, 8) < count, place, -4096)
    token = iota((TILES, ROWS), 1)
    spread = jnp.where(iota((TILES, ROWS), 0) == dv(token, 8), place, 0).astype(F32)
    target = jnp.sum(spread, axis=0, keepdims=True).astype(jnp.int32) + md(iota((1, ROWS), 1), 8)
    for to in range(8):
        picks[to] = (target == iota((128, ROWS), 0) + to * 128).astype(BF16)

    send_block(0, 3)
    send_y(1, 0)
    each(2, fc1)

    for j in range(2):
        at, off = window(s * FEAT + j * RUN)
        row, col = iota((RUNP, 384), 0), iota((RUNP, 384), 1)
        chosen = (col == row + off) & (row < RUN)
        values = dot(chosen.astype(BF16), patches[:, pl.ds(at, 384)], ((1,), (1,)))
        bias, scale = (
            jnp.sum(jnp.where(chosen, rows[i : i + 1, pl.ds(at, 384)], 0.0), axis=1, keepdims=True)
            for i in (1, 2)
        )
        base[j] = values + scale * bias
        scales[j] = scale

    send_block(0, 4)
    send_x(1, 0)
    each(3, fc1)
    each(4, fc1)

    def gelu(i, carry):
        at = pl.ds(pl.multiple_of(i * 64, 64), 64)
        pre = acc[at, :] + loc_bias[...]
        hidden[at, :] = (0.5 * pre * (1.0 + lax.erf(pre * 0.7071067811865476))).astype(BF16)
        return carry

    lax.fori_loop(0, 4, gelu, 0)
    send_block(1, 1)
    lax.fori_loop(4, 8, gelu, 0)

    each(0, fc2)
    each(1, fc2)
    each(0, sum_send)
    send_block(1, 2)
    each(1, sum_send)
    each(0, sum_relay)
    each(1, sum_relay)
    send_block(1, 3)
    each(2, fc2)
    each(2, sum_send)
    send_block(1, 4)
    each(2, sum_relay)
    each(3, fc2)
    each(4, fc2)
    each(3, sum_send)
    each(4, sum_send)

    for m in range(2):
        for k in range(2):
            for l in range(2):
                if k or l:
                    stage_copy(m, k, l).wait_send()
        pl.when(e == 1)(lambda: stage_copy(m, 0, 0).wait_send())
        for t in range(4):
            for way, piece in y_parts(t):
                y_copy(m, way, t, piece).wait_send()
        for t in range(5):
            for way in range(1 if t in (0, 4) else 2):
                for cut in range(len(x_cuts(m, t))):
                    x_copy(m, cut, block_at(way, t), t).wait_send()

    for t in range(5):
        each(t, sum_end)

    def b_copy(step, src):
        g, zp, xp = peer(step)
        return copy(turned.at[g, src], out.at[z, src, x], b_send.at[step], b_recv.at[step], dp_id(zp, y, xp))

    def b_all(step):
        g, zp, xp = peer(8 - step)
        return copy(turned.at[g], out.at[zp, :, xp], b_send.at[step], b_recv.at[step], dp_id(zp, y, xp))

    def turn(i, carry):
        odd = md(i, 2)
        src = md(2 * md(s, 4) + odd * dv(i + 1, 2) + (1 - odd) * (8 - dv(i, 2)), 8)
        step = md(y + 8 - src, 8)

        @pl.when(step > 0)
        def _():
            for j in range(2):
                a_copy(j, step, True).wait_recv()

        block = None
        for j in range(2):
            term = dot(coming[j, src], keeps[j], ((0,), (0,)))
            block = term if block is None else block + term
        turned[:, src] = block.astype(BF16).reshape(8, 16, FEAT)

        def send(step, carry):
            b_copy(step, src).start()
            return carry

        return lax.fori_loop(1, 8, send, carry)

    lax.fori_loop(0, 8, turn, 0)

    out[z, :, x] = turned[z * 4 + x]

    for step in range(1, 8):
        b_all(step).wait_recv()
    for step in range(1, 8):
        b_all(step).wait_send()
    for slot in range(4):
        pair_copy(0, slot).wait_send()
    for j in range(2):
        for way in range(2):
            side_copy(j, way).wait_send()
        for step in range(1, 8):
            a_copy(j, step).wait_send()


def local(
    patches,
    tile_counts,
    owners,
    plan,
    norm_gain,
    fc1_weight,
    fc1_bias,
    fc2_weight,
    fc2_bias,
    layer_scale,
):
    width = patches.shape[2]
    vmem = pl.BlockSpec(memory_space=pltpu.VMEM)
    smem = pl.BlockSpec(memory_space=pltpu.SMEM)
    dma = pltpu.SemaphoreType.DMA
    received = pl.pallas_call(
        kernel,
        out_shape=jax.ShapeDtypeStruct((NZ, NY, NX, 16, FEAT), BF16),
        in_specs=[pl.BlockSpec(memory_space=pl.ANY), smem, vmem, smem] + [vmem] * 6,
        out_specs=vmem,
        scratch_shapes=[
            pltpu.VMEM((ROWS, D), BF16),
            pltpu.VMEM((8, D), F32),
            pltpu.VMEM((2, SHP, FP), BF16),
            pltpu.VMEM((2, 4, SHP, FP), BF16),
            pltpu.VMEM((2, 8, 2, PACKED, 128), BF16),
            pltpu.VMEM((2 * RUNP, FP), BF16),
            pltpu.VMEM((ROWS, D), BF16),
            pltpu.VMEM((8, ROWS, 2 * RUNP), BF16),
            pltpu.VMEM((ROWS, FP), F32),
            pltpu.VMEM((1, FP), F32),
            pltpu.VMEM((ROWS, FP), BF16),
            pltpu.VMEM((8, 2, RUNP, ROWS), BF16),
            pltpu.VMEM((4, 2, RUNP, ROWS), BF16),
            pltpu.VMEM((2, RUNP, ROWS), BF16),
            pltpu.VMEM((2, 2, RUNP, TOK), BF16),
            pltpu.VMEM((2, 2, RUNP, ROWS), BF16),
            pltpu.VMEM((2, 3, RUNP, ROWS), BF16),
            pltpu.VMEM((2, RUNP, ROWS), F32),
            pltpu.VMEM((2, RUNP, 1), F32),
            pltpu.VMEM((8, 128, ROWS), BF16),
            pltpu.VMEM((2, 8, RUNP, 128), BF16),
            pltpu.VMEM((2, 8, RUNP, 128), BF16),
            pltpu.VMEM((8, 8, 16, FEAT), BF16),
            pltpu.VMEM((RUNP, 128), F32),
            pltpu.VMEM((RUNP, 64), BF16),
            pltpu.VMEM((128, 128), BF16),
            pltpu.VMEM((2, RUNP, FEAT), BF16),
            dma,
            dma((2, 4)),
            dma((2, 4)),
            dma((2, 2, 4, 2)),
            dma((2, 2, 4, 2)),
            dma((2, 3, 8)),
            dma((2, 3, 8)),
            dma((4,)),
            dma((4,)),
            dma((2, 2)),
            dma((2, 2)),
            dma((2, 3)),
            dma((2, 3)),
            dma((2, 8)),
            dma((2, 8)),
            dma((8,)),
            dma((8,)),
        ],
        compiler_params=pltpu.CompilerParams(
            collective_id=0, has_side_effects=True, vmem_limit_bytes=56 * 1024 * 1024
        ),
    )(
        patches.reshape(ROWS, width),
        tile_counts,
        owners.T,
        plan.T,
        norm_gain,
        fc1_weight,
        fc1_bias,
        fc2_weight.T,
        fc2_bias,
        layer_scale,
    )
    return received.reshape(NZ * NY * NX * 16, FEAT)


def solution(mesh):
    in_specs = (
        P("dp", None, None),
        P("dp"),
        P("dp", None),
        P(),
        P(),
        P("dp", "section"),
        P(),
        P("section", "dp"),
        P(),
        P(),
    )
    out_specs = P("dp", "section")
    return jax.shard_map(local, mesh=mesh, in_specs=in_specs, out_specs=out_specs, check_vma=False)
```
